128 devices in a mesh: grp: 2 (over core), ty: 8 (over x_lo, y), tx: 8 (over x_hi, z).
Axes of the slice: x: 4 (x_hi: 2, x_lo: 2; x = x_hi * 2 + x_lo), y: 4, z: 4, core: 2. Of those that a mesh axis runs over, the one named last changes fastest.
Arguments:
- coupled_state: float32 [2, 23, 32, 16, 1024], P('grp', None, None, 'ty', 'tx'), may hold values from -4 to 4, as said below
- land_mask: int32 [16, 1024], P('ty', 'tx'), may hold values 0 or 1
- bottom_level: int32 [16, 1024], P('ty', 'tx'), may hold values from 1 to 32
- shortwave: float32 [16, 1024], P('ty', 'tx'), may hold values from 0.5 to 1.5
- absorb: float32 [19], replicated, may hold values from 0.01 to 0.1
- reaction: float32 [19, 19], replicated, may hold values from -1.25 to 1.25
Outputs:
- new_state: float32 [2, 23, 32, 16, 1024], P('grp', None, None, 'ty', 'tx')
The draws below stay inside these ranges and needn't reach their ends.
Inputs may be any that keep to these rules, and one draw needn't show every extreme that they name: `coupled_state`: fields 0 and 1 lie in -2 to 2, fields 2 and 3 in -4 to 4, the tracers in 0.1 to 2.
All inputs are finite; a program needn't handle non-finite values. No bound on the sum of `land_mask` on one device may be relied on, other than what follows from the above.
Results may differ from the reference program's by a relative error of at most 0.0003.
Values sent between devices are 32-bit elements; how exact they have to be, the bound alone decides.
A program may use at most 192 MiB of HBM per device.

```python
import math
import jax
import jax.numpy as jnp
from jax import lax

NTR = 19
NZ = 32
STEPS = 2
NX = 16
NY = 1024


def draw_coupled_state(key, part):
    flow_key, scalar_key, tracer_key = jax.random.split(jax.random.fold_in(key, 17), 3)
    pair_shape = (2, 2, NZ, NX, NY)
    tracer_shape = (2, NTR, NZ, NX, NY)
    flow = jnp.clip(0.8 * jax.random.normal(flow_key, pair_shape, jnp.float32), -2.0, 2.0)
    scalars = jnp.clip(jax.random.normal(scalar_key, pair_shape, jnp.float32), -4.0, 4.0)
    tracers = jnp.exp(jax.random.uniform(tracer_key, tracer_shape, jnp.float32, math.log(0.1), math.log(2.0)))
    return jnp.concatenate([flow, scalars, tracers], axis=1)


def set_ends(values, own_key, low, high):
    extent = values.shape
    spot = [jax.random.randint(jax.random.fold_in(own_key, axis), (), 0, extent[axis]) for axis in range(len(extent))]
    values = values.at[tuple(spot)].set(low)
    longest = extent.index(max(extent))
    spot[longest] = (spot[longest] + 1) % extent[longest]
    return values.at[tuple(spot)].set(high)


def block_levels(key, extent, cuts, low, high):
    def one(axis_at, blocks):
        draws = jax.random.uniform(jax.random.fold_in(jax.random.fold_in(key, 6), axis_at), (blocks,), jnp.float32, low / len(cuts), high / len(cuts))
        return jnp.repeat(jnp.exp(draws), extent[axis_at] // blocks).reshape((-1,) + (1,) * (len(extent) - axis_at - 1))

    level = one(*cuts[0])
    for cut in cuts[1:]:
        level = level * one(*cut)
    return level


def bell_draw(rng, dims, width, bound, kind=jnp.bfloat16):
    return jnp.clip(width * jax.random.normal(rng, dims, jnp.float32), -bound, bound).astype(kind)


def setup_inputs(seed: int = 0) -> dict:
    splits = jax.random.split(jax.random.key(seed), 7)
    coupled_state = draw_coupled_state(jax.random.fold_in(splits[6], 71), 0)
    land_mask = set_ends((jax.random.randint(splits[1], (NX, NY), 0, 6) < 5).astype(jnp.int32), jax.random.fold_in(splits[1], 1), 0, 1)
    bottom_level = set_ends(jax.random.randint(splits[2], (NX, NY), 1, NZ + 1), jax.random.fold_in(splits[2], 1), 1, NZ).astype(jnp.int32)
    shortwave = jnp.clip(0.5 + 1.0 * jax.random.uniform(splits[3], (NX, NY), jnp.float32) ** block_levels(splits[3], (NX, NY), ((0, 8), (1, 8)), -0.2, 0.2), 0.5, 1.5)
    absorb = jnp.clip(jnp.exp(jax.random.uniform(splits[4], (NTR,), jnp.float32, math.log(0.01), math.log(0.1))), 0.01, 0.1)
    reaction = bell_draw(splits[5], (NTR, NTR), NTR ** -0.5, 1.25, jnp.float32)
    return dict(coupled_state=coupled_state, land_mask=land_mask, bottom_level=bottom_level, shortwave=shortwave, absorb=absorb, reaction=reaction)


integration_interval = 0.1
tracer_step = 0.08
coriolis = 0.8
barotropic_gradient_coefficient = 0.1
water_extinction = 0.04
layer_depth = 0.05
growth_peak = 2.0
half_light = 0.5
ratio_floor = 0.01


def east_of(values):
    zero_rim = jnp.zeros_like(values[..., :1, :])
    return jnp.concatenate([values[..., 1:, :], zero_rim], axis=-2)


def west_of(values):
    zero_rim = jnp.zeros_like(values[..., :1, :])
    return jnp.concatenate([zero_rim, values[..., :-1, :]], axis=-2)


def north_of(values):
    zero_rim = jnp.zeros_like(values[..., :1])
    return jnp.concatenate([values[..., 1:], zero_rim], axis=-1)


def south_of(values):
    zero_rim = jnp.zeros_like(values[..., :1])
    return jnp.concatenate([zero_rim, values[..., :-1]], axis=-1)


def diffusion_stencil(values):
    return east_of(values) + west_of(values) + north_of(values) + south_of(values) - 4.0 * values


def light_field(tracers, absorb, shortwave):
    extinction = water_extinction + jnp.einsum("t,tkxy->kxy", absorb, tracers, precision=lax.Precision.HIGHEST)
    optical = jnp.cumsum(extinction, axis=0) * layer_depth
    light_below = shortwave * jnp.exp(-optical)
    light_above = light_below * jnp.exp(layer_depth * extinction)
    return light_below, light_above


def ocean_update(gridded_quantities, marine_indicator, absorb, shortwave):
    zonal_current, meridional_current, thermal_state, brine_content = gridded_quantities[0], gridded_quantities[1], gridded_quantities[2], gridded_quantities[3]
    hydrostatic_load = jnp.cumsum(-0.2 * thermal_state + 0.8 * brine_content, axis=0) * barotropic_gradient_coefficient
    grad_east = 0.5 * (east_of(hydrostatic_load) - west_of(hydrostatic_load))
    grad_north = 0.5 * (north_of(hydrostatic_load) - south_of(hydrostatic_load))
    zonal_current_later = marine_indicator * (zonal_current + integration_interval * (coriolis * meridional_current - grad_east + diffusion_stencil(zonal_current)))
    meridional_current_later = marine_indicator * (meridional_current + integration_interval * (-coriolis * zonal_current - grad_north + diffusion_stencil(meridional_current)))
    light_below, light_above = light_field(gridded_quantities[4:], absorb, shortwave)
    thermal_forcing = (light_above - light_below) / layer_depth
    thermal_state_later = marine_indicator * (thermal_state + integration_interval * (diffusion_stencil(thermal_state) + thermal_forcing))
    brine_content_later = marine_indicator * (brine_content + integration_interval * diffusion_stencil(brine_content))
    return jnp.stack([zonal_current_later, meridional_current_later, thermal_state_later, brine_content_later])


def tracer_fluxes(gridded_quantities, inside):
    tracers = gridded_quantities[4:]
    face_east = 0.5 * (gridded_quantities[0] + east_of(gridded_quantities[0])) * inside * east_of(inside)
    face_north = 0.5 * (gridded_quantities[1] + north_of(gridded_quantities[1])) * inside * north_of(inside)
    tracer_east = east_of(tracers)
    tracer_north = north_of(tracers)
    low_east = jnp.maximum(face_east, 0.0) * tracers + jnp.minimum(face_east, 0.0) * tracer_east
    low_north = jnp.maximum(face_north, 0.0) * tracers + jnp.minimum(face_north, 0.0) * tracer_north
    anti_east = 0.5 * face_east * (tracers + tracer_east) - low_east
    anti_north = 0.5 * face_north * (tracers + tracer_north) - low_north
    lowered = tracers - tracer_step * (low_east - west_of(low_east) + low_north - south_of(low_north))
    tracer_west = west_of(tracers)
    tracer_south = south_of(tracers)
    bound_up = jnp.maximum(jnp.maximum(jnp.maximum(tracers, tracer_east), jnp.maximum(tracer_west, tracer_north)), tracer_south)
    bound_down = jnp.minimum(jnp.minimum(jnp.minimum(tracers, tracer_east), jnp.minimum(tracer_west, tracer_north)), tracer_south)
    west_anti = west_of(anti_east)
    south_anti = south_of(anti_north)
    gain_in = jnp.maximum(west_anti, 0.0) - jnp.minimum(anti_east, 0.0) + jnp.maximum(south_anti, 0.0) - jnp.minimum(anti_north, 0.0)
    gain_out = jnp.maximum(anti_east, 0.0) - jnp.minimum(west_anti, 0.0) + jnp.maximum(anti_north, 0.0) - jnp.minimum(south_anti, 0.0)
    room_up = jnp.maximum(bound_up - lowered, 0.0) / tracer_step
    room_down = jnp.maximum(lowered - bound_down, 0.0) / tracer_step
    ratio_in = jnp.minimum(gain_in, room_up) / jnp.maximum(gain_in, ratio_floor)
    ratio_out = jnp.minimum(gain_out, room_down) / jnp.maximum(gain_out, ratio_floor)
    return lowered, anti_east, anti_north, jnp.stack([ratio_in, ratio_out])


def tracer_finish(gridded_quantities, lowered, anti_east, anti_north, ratios, marine_indicator, absorb, shortwave, reaction):
    ratio_in, ratio_out = ratios[0], ratios[1]
    limit_east = jnp.where(anti_east >= 0.0, jnp.minimum(east_of(ratio_in), ratio_out), jnp.minimum(ratio_in, east_of(ratio_out)))
    limit_north = jnp.where(anti_north >= 0.0, jnp.minimum(north_of(ratio_in), ratio_out), jnp.minimum(ratio_in, north_of(ratio_out)))
    flux_east = limit_east * anti_east
    flux_north = limit_north * anti_north
    advected = lowered - tracer_step * (flux_east - west_of(flux_east) + flux_north - south_of(flux_north))
    light_below, light_above = light_field(advected, absorb, shortwave)
    growth = growth_peak * jnp.exp(0.063 * gridded_quantities[2]) * light_below / (light_below + half_light) * (1.0 + 0.2 * jnp.tanh(gridded_quantities[3]))
    mixed_terms = jnp.einsum("st,tkxy->skxy", reaction, advected, precision=lax.Precision.HIGHEST)
    return marine_indicator * (advected + tracer_step * growth * mixed_terms)


def reference(coupled_state, land_mask, bottom_level, shortwave, absorb, reaction):
    levels = jnp.arange(NZ, dtype=jnp.int32)[:, None, None]
    marine_indicator = ((land_mask[None] == 1) & (levels < bottom_level[None])).astype(jnp.float32)
    inside = jnp.ones((NX, NY), jnp.float32)
    ocean_view = coupled_state[0]
    tracer_view = coupled_state[1]
    for step_index in range(STEPS):
        dynamics = ocean_update(ocean_view, marine_indicator, absorb, shortwave)
        lowered, anti_east, anti_north, ratios = tracer_fluxes(tracer_view, inside)
        tracers = tracer_finish(tracer_view, lowered, anti_east, anti_north, ratios, marine_indicator, absorb, shortwave, reaction)
        if step_index + 1 < STEPS:
            ocean_view = jnp.concatenate([dynamics, tracers], axis=0)
            tracer_view = ocean_view
        else:
            ocean_view = jnp.concatenate([dynamics, ocean_view[4:]], axis=0)
            tracer_view = jnp.concatenate([tracer_view[:4], tracers], axis=0)
    return jnp.stack([ocean_view, tracer_view])
```

```python
import functools

import jax
import jax.numpy as jnp
from jax import lax
from jax.experimental import pallas as pl
from jax.experimental.pallas import tpu as pltpu
from jax.sharding import PartitionSpec as P

STEPS = 2
NF = 23
NT = 19
NZ = 32
CH = 8
NK = NZ // CH
MESH = pl.DeviceIdType.MESH
F32 = jnp.float32

integration_interval = 0.1
tracer_step = 0.08
coriolis = 0.8
barotropic_gradient_coefficient = 0.1
water_extinction = 0.04
layer_depth = 0.05
growth_peak = 2.0
half_light = 0.5
ratio_floor = 0.01

DIAGS = ((-1, -1), (-1, 1), (1, -1), (1, 1))


def lanes(shape):
    return lax.broadcasted_iota(jnp.int32, shape, len(shape) - 1)


def roll(x, shift):
    return pltpu.roll(x, shift % 128 if isinstance(shift, int) else shift, x.ndim - 1)


def cumulative(x):
    n = x.shape[0]
    level = lax.broadcasted_iota(jnp.int32, x.shape, 0)
    d = 1
    while d < n:
        x = x + jnp.where(level >= d, pltpu.roll(x, d, 0), 0.0)
        d *= 2
    return x


def inverse(x):
    r = pl.reciprocal(x, approx=True)
    return r * (2.0 - x * r)


def kernel(
    x, land, bottom, shortwave, absorb, reaction, out,
    V, H, PS, PT, PD, ADV, CO, ZC, ZS, D, DH, SS, ST, KD,
    lsem, row_s, row_r, col_s, col_r, diag_s, diag_r, dyn_s, dyn_r, tra_s, tra_r, ors, orr, ocs, ocr,
):
    grp, ty, tx = lax.axis_index("grp"), lax.axis_index("ty"), lax.axis_index("tx")
    nty, ntx = lax.axis_size("ty"), lax.axis_size("tx")
    has_y = (ty > 0, ty < nty - 1)
    has_x = (tx > 0, tx < ntx - 1)
    step_of = (-1, 1)

    def has_diag(i):
        a, b = DIAGS[i]
        return has_y[(a + 1) // 2] & has_x[(b + 1) // 2]

    barrier = pltpu.get_barrier_semaphore()
    count = jnp.int32(1)
    pl.semaphore_signal(barrier, inc=1, device_id={"grp": 1 - grp}, device_id_type=MESH)
    for d in range(2):
        count = count + has_y[d].astype(jnp.int32) + has_x[d].astype(jnp.int32)

        @pl.when(has_y[d])
        def _():
            pl.semaphore_signal(barrier, inc=1, device_id={"ty": ty + step_of[d]}, device_id_type=MESH)

        @pl.when(has_x[d])
        def _():
            pl.semaphore_signal(barrier, inc=1, device_id={"tx": tx + step_of[d]}, device_id_type=MESH)

    load = pltpu.make_async_copy(x, V.at[0], lsem.at[0])
    load.start()

    def fill(ref, n):
        def body(i, c):
            ref[i] = jnp.zeros(ref.shape[1:], F32)
            return c

        lax.fori_loop(0, n, body, 0)

    lane8 = lanes((CH, 128))
    four8 = lane8 % 4
    first, last = lane8 == 0, lane8 == 127

    def tracer_side():
        n_diag = jnp.int32(0)
        for i in range(4):
            n_diag = n_diag + has_diag(i).astype(jnp.int32)

            @pl.when(has_diag(i))
            def _():
                a, b = DIAGS[i]
                pl.semaphore_signal(barrier, inc=1, device_id={"ty": ty + a, "tx": tx + b}, device_id_type=MESH)

            @pl.when(jnp.logical_not(has_diag(i)))
            def _():
                for s in range(STEPS):
                    PD[s, i] = jnp.zeros(PD.shape[2:], F32)

        for d in range(2):
            @pl.when(jnp.logical_not(has_y[d]))
            def _():
                for s in range(STEPS):
                    fill(H.at[s, d], NF)

            @pl.when(jnp.logical_not(has_x[d]))
            def _():
                for s in range(STEPS):
                    fill(PT.at[s, d], 2)

        def row_copy(s, d, k, part):
            lo, n = ((0, 2), (4, NT))[part]
            rows = pl.ds(pl.multiple_of(k * 16, 16), 16)
            src = (x if s == 0 else V.at[s]).at[pl.ds(lo, n), rows]
            return pltpu.make_async_remote_copy(
                src_ref=src,
                dst_ref=H.at[s, 1 - d, pl.ds(lo, n), rows],
                send_sem=row_s.at[s, d, k, part],
                recv_sem=row_r.at[s, 1 - d, k, part],
                device_id={"ty": ty + step_of[d]},
                device_id_type=MESH,
            )

        def row_arrival(s, d, k, part):
            lo, n = ((0, 2), (4, NT))[part]
            rows = pl.ds(pl.multiple_of(k * 16, 16), 16)
            return pltpu.make_async_remote_copy(
                src_ref=V.at[s, pl.ds(lo, n), rows],
                dst_ref=H.at[s, d, pl.ds(lo, n), rows],
                send_sem=row_s.at[s, d, k, part],
                recv_sem=row_r.at[s, d, k, part],
                device_id={"ty": ty + step_of[d]},
                device_id_type=MESH,
            )

        def col_copy(s, d, k, arrival=False):
            lev = pl.ds(pl.multiple_of(k * CH, CH), CH)
            to = d if arrival else 1 - d
            return pltpu.make_async_remote_copy(
                src_ref=PS.at[s, :, lev],
                dst_ref=PT.at[s, to, :, lev],
                send_sem=col_s.at[s, d, k],
                recv_sem=col_r.at[s, to, k],
                device_id={"tx": tx + step_of[d]},
                device_id_type=MESH,
            )

        def diag_copy(s, i, k, arrival=False):
            a, b = DIAGS[i]
            lev = pl.ds(pl.multiple_of(k * CH, CH), CH)
            to = i if arrival else 3 - i
            return pltpu.make_async_remote_copy(
                src_ref=PS.at[s, (a + 1) // 2, lev],
                dst_ref=PD.at[s, to, lev],
                send_sem=diag_s.at[s, i, k],
                recv_sem=diag_r.at[s, to, k],
                device_id={"ty": ty + a, "tx": tx + b},
                device_id_type=MESH,
            )

        def each_row(s, k, act):
            for d in range(2):
                @pl.when(has_y[d])
                def _():
                    for part in range(2):
                        act(s, d, k, part)

        def send_rows(s, k):
            each_row(s, k, lambda *a: row_copy(*a).start())

        def send_edges(s, k):
            for d in range(2):
                @pl.when(has_x[d])
                def _():
                    col_copy(s, d, k).start()
            for i in range(4):
                @pl.when(has_diag(i))
                def _():
                    diag_copy(s, i, k).start()

        def receive(s, k):
            for d in range(2):
                @pl.when(has_x[d])
                def _():
                    col_copy(s, d, k, True).wait_recv()
            for i in range(4):
                @pl.when(has_diag(i))
                def _():
                    diag_copy(s, i, k, True).wait_recv()
            each_row(s, k, lambda *a: row_arrival(*a).wait_recv())

        def sent(s, k):
            each_row(s, k, lambda *a: row_copy(*a).wait_send())
            for d in range(2):
                @pl.when(has_x[d])
                def _():
                    col_copy(s, d, k).wait_send()
            for i in range(4):
                @pl.when(has_diag(i))
                def _():
                    diag_copy(s, i, k).wait_send()

        def tracers_over(k):
            rows = pl.ds(pl.multiple_of(k * 16, 16), 16)
            return pltpu.make_async_remote_copy(
                src_ref=V.at[1, pl.ds(4, NT), rows],
                dst_ref=V.at[2, pl.ds(4, NT), rows],
                send_sem=tra_s.at[k],
                recv_sem=tra_r.at[k],
                device_id={"grp": 1 - grp},
                device_id_type=MESH,
            )

        def store_out(k):
            rows = pl.ds(pl.multiple_of(k * 16, 16), 16)
            return pltpu.make_async_copy(V.at[2, pl.ds(4, NT), rows], out.at[pl.ds(4, NT), rows], lsem.at[1 + k])

        def pack(s, start, count):
            lane = lanes((count, 128))
            quarter = lane // 4

            def body(f, rows):
                shift = 4 * f + 2
                return tuple(
                    jnp.where(quarter == f, roll(V[s, f, pl.ds(2 * start + r, count, 2), :], shift), rows[r])
                    for r in range(2)
                )

            zero = jnp.zeros((count, 128), F32)
            packed = lax.fori_loop(0, NF, body, (zero, zero))
            for r in range(2):
                PS[s, r, pl.ds(start, count), :] = packed[r]

        def chunk(s, k, carry):
            base = k * 16
            lev = pl.ds(pl.multiple_of(k * CH, CH), CH)

            def row(f, r):
                at = pl.ds(base + r % 2, CH, 2)
                if r < 0:
                    return H[s, 0, f, at, :]
                if r > 1:
                    return H[s, 1, f, at, :]
                return V[s, f, at, :]

            y_lo = jnp.where(has_y[0], 0.02, 0.0).astype(F32)
            y_hi = jnp.where(has_y[1], 0.02, 0.0).astype(F32)
            x_lo = jnp.where(has_x[0], 0.02, 0.0).astype(F32)
            x_hi = jnp.where(has_x[1], 0.02, 0.0).astype(F32)
            right = four8 == 1
            left = four8 == 2

            own = [PS[s, r, lev, :] for r in range(2)]
            low = [PD[s, 0, lev, :], PT[s, 0, 0, lev, :], PT[s, 0, 1, lev, :], PD[s, 2, lev, :]]
            high = [PD[s, 1, lev, :], PT[s, 1, 0, lev, :], PT[s, 1, 1, lev, :], PD[s, 3, lev, :]]
            mid = [jnp.where(right, roll(high[i], -1), roll(low[i], 1)) for i in range(4)]
            for i in range(4):
                ZC[i] = mid[i]
            north = [jnp.where(right, roll(high[1 + r], -2), own[r]) for r in range(2)]
            south = [jnp.where(right, own[r], roll(low[1 + r], 2)) for r in range(2)]

            def spread(value, f):
                value = jnp.where(lane8 // 4 == f, value, 0.0)
                for d in (4, 8, 16, 32, 64):
                    value = value + roll(value, d)
                return value

            def face(q, a, b):
                anti = jnp.abs(q) * (b - a)
                return anti, q * (a + b) - anti

            def bounds(centre, others):
                hi = lo = centre
                for o in others:
                    hi, lo = jnp.maximum(hi, o), jnp.minimum(lo, o)
                return hi, lo

            def gains(w, e, n, so):
                gain_in = (jnp.maximum(w, 0.0) - jnp.minimum(e, 0.0)) + (jnp.maximum(so, 0.0) - jnp.minimum(n, 0.0))
                gain_out = (jnp.maximum(e, 0.0) - jnp.minimum(w, 0.0)) + (jnp.maximum(n, 0.0) - jnp.minimum(so, 0.0))
                return gain_in, gain_out

            def ratio(gain, room):
                return jnp.minimum(gain, jnp.maximum(room, 0.0)) * inverse(
                    jnp.maximum(gain, ratio_floor * tracer_step)
                )

            u_mid = [spread(m, 0) for m in mid]
            q_rows = [
                (u_mid[0] + u_mid[1]) * y_lo,
                (u_mid[1] + u_mid[2]) * 0.02,
                (u_mid[2] + u_mid[3]) * y_hi,
            ]
            faces = [face(q_rows[i], mid[i], mid[i + 1]) for i in range(3)]
            for r in range(2):
                v_mid = spread(mid[1 + r], 1)
                q_n = (v_mid + spread(north[r], 1)) * jnp.where(left, x_lo, 0.02)
                q_s = (v_mid + spread(south[r], 1)) * jnp.where(right, x_hi, 0.02)
                a_n, l_n = face(q_n, mid[1 + r], north[r])
                a_s, l_s = face(q_s, south[r], mid[1 + r])
                a_w, l_w = faces[r]
                a_e, l_e = faces[r + 1]
                lowered = mid[1 + r] - (l_e - l_w + l_n - l_s)
                hi, lo = bounds(mid[1 + r], (mid[r], mid[2 + r], north[r], south[r]))
                gain_in, gain_out = gains(a_w, a_e, a_n, a_s)
                take_in = (right & (a_s >= 0.0)) | (jnp.logical_not(right) & (a_n < 0.0))
                gain = jnp.where(take_in, gain_in, gain_out)
                room = jnp.where(take_in, hi - lowered, lowered - lo)
                ZS[r] = ratio(gain, room)

            u = [row(0, r) for r in range(-2, 4)]
            for i, scale in enumerate((0.02, y_lo, 0.02, y_hi, 0.02)):
                CO[i] = (u[i] + u[i + 1]) * scale
            for i in range(4):
                v = row(1, i - 1)
                side = roll(mid[i], 126 - 4)
                CO[5 + i] = (v + jnp.where(last, side, roll(v, -1))) * jnp.where(last, x_hi, 0.02)
                CO[9 + i] = (v + jnp.where(first, side, roll(v, 1))) * jnp.where(first, x_lo, 0.02)

            def transport(t, extinction):
                f = t + 4
                c = [row(f, r) for r in range(-2, 4)]
                turn = 126 - 4 * f
                fe = [face(CO[i], c[i], c[i + 1]) for i in range(5)]
                lowered, ratio_in, ratio_out, an, as_ = {}, {}, {}, {}, {}
                for i in range(1, 5):
                    side = roll(ZC[i - 1], turn)
                    c_n = jnp.where(last, side, roll(c[i], -1))
                    c_s = jnp.where(first, side, roll(c[i], 1))
                    a_n, l_n = face(CO[4 + i], c[i], c_n)
                    a_s, l_s = face(CO[8 + i], c_s, c[i])
                    a_w, l_w = fe[i - 1]
                    a_e, l_e = fe[i]
                    low_c = c[i] - (l_e - l_w + l_n - l_s)
                    hi, lo = bounds(c[i], (c[i - 1], c[i + 1], c_n, c_s))
                    gain_in, gain_out = gains(a_w, a_e, a_n, a_s)
                    room_in, room_out = hi - low_c, low_c - lo
                    if i in (1, 4):
                        take_in = a_e < 0.0 if i == 1 else a_w >= 0.0
                        ratio_in[i] = ratio(
                            jnp.where(take_in, gain_in, gain_out), jnp.where(take_in, room_in, room_out)
                        )
                    else:
                        lowered[i], an[i], as_[i] = low_c, a_n, a_s
                        ratio_in[i] = ratio(gain_in, room_in)
                        ratio_out[i] = ratio(gain_out, room_out)
                a = fe[1][0]
                f_lo = a * jnp.minimum(ratio_in[1], jnp.where(a >= 0.0, ratio_in[2], ratio_out[2]))
                a = fe[2][0]
                f_mid = a * jnp.where(
                    a >= 0.0,
                    jnp.minimum(ratio_in[3], ratio_out[2]),
                    jnp.minimum(ratio_in[2], ratio_out[3]),
                )
                a = fe[3][0]
                f_hi = a * jnp.minimum(jnp.where(a >= 0.0, ratio_out[3], ratio_in[3]), ratio_in[4])
                result = []
                for i, f_w, f_e in ((2, f_lo, f_mid), (3, f_mid, f_hi)):
                    side = roll(ZS[i - 2], turn)
                    a_n, a_s = an[i], as_[i]
                    up = a_n >= 0.0
                    mine = jnp.where(up, ratio_out[i], ratio_in[i])
                    other = jnp.where(up, roll(ratio_in[i], -1), roll(ratio_out[i], -1))
                    f_n = a_n * jnp.minimum(mine, jnp.where(last, side, other))
                    at_rim = a_s * jnp.minimum(side, jnp.where(a_s >= 0.0, ratio_in[i], ratio_out[i]))
                    f_s = jnp.where(first, at_rim, roll(f_n, 1))
                    advected = lowered[i] - (f_e - f_w + f_n - f_s)
                    ADV[t, i - 2] = advected
                    result.append(extinction[i - 2] + absorb[t] * advected)
                return tuple(result)

            base_light = jnp.full((CH, 128), water_extinction, F32)
            extinction = lax.fori_loop(0, NT, transport, (base_light, base_light))

            level = k * CH + lax.broadcasted_iota(jnp.int32, (CH, 128), 0)
            wet, growth, carries = [], [], []
            for r in range(2):
                total = cumulative(extinction[r]) + carry[r]
                carries.append(carry[r] + jnp.sum(extinction[r], axis=0, keepdims=True))
                below = shortwave[pl.ds(r, 1), :] * jnp.exp(-layer_depth * total)
                sea = (land[pl.ds(r, 1), :] == 1) & (level < bottom[pl.ds(r, 1), :])
                wet.append(jnp.where(sea, 1.0, 0.0))
                grow = (
                    growth_peak
                    * jnp.exp(0.063 * row(2, r))
                    * below
                    / (below + half_light)
                    * (1.0 + 0.2 * jnp.tanh(row(3, r)))
                )
                growth.append(wet[r] * (tracer_step * grow))

            def react(o, c):
                for r in range(2):
                    mixed = reaction[o, 0] * ADV[0, r]
                    for t in range(1, NT):
                        mixed = mixed + reaction[o, t] * ADV[t, r]
                    V[s + 1, o + 4, pl.ds(base + r, CH, 2), :] = wet[r] * ADV[o, r] + growth[r] * mixed
                return c

            lax.fori_loop(0, NT, react, 0)
            return tuple(carries)

        dynamics_in = pltpu.make_async_remote_copy(
            src_ref=V.at[1, pl.ds(0, 4)],
            dst_ref=V.at[1, pl.ds(0, 4)],
            send_sem=dyn_s,
            recv_sem=dyn_r,
            device_id={"grp": 1 - grp},
            device_id_type=MESH,
        )
        dynamics_out = pltpu.make_async_copy(V.at[1, pl.ds(0, 4)], out.at[pl.ds(0, 4)], lsem.at[0])

        load.wait()
        pack(0, 0, NZ)
        pl.semaphore_wait(barrier, count + n_diag)

        def begin(k, c):
            send_rows(0, k)
            send_edges(0, k)
            return c

        lax.fori_loop(0, NK, begin, 0)

        zero = jnp.zeros((1, 128), F32)

        def first_step(k, carry):
            receive(0, k)
            carry = chunk(0, k, carry)

            @pl.when(k == 0)
            def _():
                dynamics_in.wait_recv()
                dynamics_out.start()

            send_rows(1, k)
            pack(1, k * CH, CH)
            send_edges(1, k)
            tracers_over(k).start()
            return carry

        lax.fori_loop(0, NK, first_step, (zero, zero))

        def second_step(k, carry):
            receive(1, k)
            carry = chunk(1, k, carry)
            store_out(k).start()
            return carry

        lax.fori_loop(0, NK, second_step, (zero, zero))

        def finish(k, c):
            sent(0, k)
            sent(1, k)
            tracers_over(k).wait_send()
            store_out(k).wait()
            return c

        lax.fori_loop(0, NK, finish, 0)
        dynamics_out.wait()

    def ocean_side():
        for d in range(2):
            @pl.when(jnp.logical_not(has_y[d]))
            def _():
                for s in range(STEPS):
                    fill(DH.at[s, d], 4)

            @pl.when(jnp.logical_not(has_x[d]))
            def _():
                for s in range(STEPS):
                    fill(ST.at[s, d], 2)

        lane = lanes((NZ, 128))
        four, quarter = lane % 4, lane // 4
        first_z, last_z = lane == 0, lane == 127

        def row_copy(s, d, arrival=False):
            to = d if arrival else 1 - d
            return pltpu.make_async_remote_copy(
                src_ref=D.at[s, d],
                dst_ref=DH.at[s, to],
                send_sem=ors.at[s, d],
                recv_sem=orr.at[s, to],
                device_id={"ty": ty + step_of[d]},
                device_id_type=MESH,
            )

        def col_copy(s, d, arrival=False):
            to = d if arrival else 1 - d
            return pltpu.make_async_remote_copy(
                src_ref=SS.at[s],
                dst_ref=ST.at[s, to],
                send_sem=ocs.at[s, d],
                recv_sem=ocr.at[s, to],
                device_id={"tx": tx + step_of[d]},
                device_id_type=MESH,
            )

        def exchange(s, act):
            for d in range(2):
                @pl.when(has_y[d])
                def _():
                    act(row_copy, s, d)

                @pl.when(has_x[d])
                def _():
                    act(col_copy, s, d)

        def pack(s):
            for r in range(2):
                packed = jnp.zeros((NZ, 128), F32)
                for f in range(4):
                    packed = jnp.where(quarter == f, roll(D[s, r, f], 4 * f + 2), packed)
                SS[s, r] = packed

        def light(ref):
            def body(t, acc):
                return acc + absorb[t] * ref[t + 4]

            KD[...] = lax.fori_loop(0, NT, body, jnp.full((2 * NZ, 128), water_extinction, F32))

        def update(s):
            level = lax.broadcasted_iota(jnp.int32, (NZ, 128), 0)
            for r in range(2):
                side = jnp.where(four == 1, roll(ST[s, 1, r], -1), roll(ST[s, 0, r], 1))
                own, lap, e_w, n_s = [], [], [], []
                for f in range(4):
                    c = D[s, r, f]
                    w = DH[s, 0, f] if r == 0 else D[s, 0, f]
                    e = DH[s, 1, f] if r == 1 else D[s, 1, f]
                    rim = roll(side, 126 - 4 * f)
                    n = jnp.where(last_z, rim, roll(c, -1))
                    so = jnp.where(first_z, rim, roll(c, 1))
                    own.append(c)
                    lap.append((e + w + n + so) - 4.0 * c)
                    e_w.append(e - w)
                    n_s.append(n - so)
                half = 0.5 * barotropic_gradient_coefficient
                grad_east = cumulative((-0.2 * e_w[2] + 0.8 * e_w[3]) * half)
                grad_north = cumulative((-0.2 * n_s[2] + 0.8 * n_s[3]) * half)
                extinction = KD[pl.ds(r, NZ, 2), :]
                below = shortwave[pl.ds(r, 1), :] * jnp.exp(-layer_depth * cumulative(extinction))
                above = below * jnp.exp(layer_depth * extinction)
                sea = (land[pl.ds(r, 1), :] == 1) & (level < bottom[pl.ds(r, 1), :])
                wet = jnp.where(sea, 1.0, 0.0)
                step = integration_interval
                new = (
                    own[0] + step * (coriolis * own[1] - grad_east + lap[0]),
                    own[1] + step * (-coriolis * own[0] - grad_north + lap[1]),
                    own[2] + step * (lap[2] + (above - below) / layer_depth),
                    own[3] + step * lap[3],
                )
                for f in range(4):
                    value = wet * new[f]
                    V[s + 1, f, pl.ds(r, NZ, 2), :] = value
                    if s + 1 < STEPS:
                        D[s + 1, r, f] = value

        dynamics_over = pltpu.make_async_remote_copy(
            src_ref=V.at[1, pl.ds(0, 4)],
            dst_ref=V.at[1, pl.ds(0, 4)],
            send_sem=dyn_s,
            recv_sem=dyn_r,
            device_id={"grp": 1 - grp},
            device_id_type=MESH,
        )

        def tracers_in(k):
            rows = pl.ds(pl.multiple_of(k * 16, 16), 16)
            return pltpu.make_async_remote_copy(
                src_ref=V.at[1, pl.ds(4, NT), rows],
                dst_ref=V.at[2, pl.ds(4, NT), rows],
                send_sem=tra_s.at[k],
                recv_sem=tra_r.at[k],
                device_id={"grp": 1 - grp},
                device_id_type=MESH,
            )

        load.wait()
        for r in range(2):
            for f in range(4):
                D[0, r, f] = V[0, f, pl.ds(r, NZ, 2), :]
        pack(0)
        pl.semaphore_wait(barrier, count)
        exchange(0, lambda copy, s, d: copy(s, d).start())
        light(V.at[0])
        exchange(0, lambda copy, s, d: copy(s, d, True).wait_recv())
        update(0)
        dynamics_over.start()
        pack(1)
        exchange(1, lambda copy, s, d: copy(s, d).start())

        def tracers_out(k):
            rows = pl.ds(pl.multiple_of(k * 16, 16), 16)
            return pltpu.make_async_copy(V.at[2, pl.ds(4, NT), rows], out.at[pl.ds(4, NT), rows], lsem.at[1 + k])

        def arrive(k, c):
            tracers_in(k).wait_recv()
            tracers_out(k).start()
            return c

        lax.fori_loop(0, NK, arrive, 0)
        light(V.at[2])
        exchange(1, lambda copy, s, d: copy(s, d, True).wait_recv())
        update(1)
        dynamics_out = pltpu.make_async_copy(V.at[2, pl.ds(0, 4)], out.at[pl.ds(0, 4)], lsem.at[0])
        dynamics_out.start()
        exchange(0, lambda copy, s, d: copy(s, d).wait_send())
        exchange(1, lambda copy, s, d: copy(s, d).wait_send())
        dynamics_over.wait_send()

        def finish(k, c):
            tracers_out(k).wait()
            return c

        lax.fori_loop(0, NK, finish, 0)
        dynamics_out.wait()

    pl.when(grp == 1)(tracer_side)
    pl.when(grp == 0)(ocean_side)


def local(coupled_state, land_mask, bottom_level, shortwave, absorb, reaction):
    x = coupled_state.reshape(NF, 2 * NZ, 128)
    vmem, smem, anywhere = (
        pl.BlockSpec(memory_space=pltpu.VMEM),
        pl.BlockSpec(memory_space=pltpu.SMEM),
        pl.BlockSpec(memory_space=pl.ANY),
    )
    dma = pltpu.SemaphoreType.DMA
    y = pl.pallas_call(
        kernel,
        out_shape=jax.ShapeDtypeStruct((NF, 2 * NZ, 128), F32),
        in_specs=[anywhere, vmem, vmem, vmem, smem, smem],
        out_specs=anywhere,
        scratch_shapes=[
            pltpu.VMEM((STEPS + 1, NF, 2 * NZ, 128), F32),
            pltpu.VMEM((STEPS, 2, NF, 2 * NZ, 128), F32),
            pltpu.VMEM((STEPS, 2, NZ, 128), F32),
            pltpu.VMEM((STEPS, 2, 2, NZ, 128), F32),
            pltpu.VMEM((STEPS, 4, NZ, 128), F32),
            pltpu.VMEM((NT, 2, CH, 128), F32),
            pltpu.VMEM((13, CH, 128), F32),
            pltpu.VMEM((4, CH, 128), F32),
            pltpu.VMEM((2, CH, 128), F32),
            pltpu.VMEM((STEPS, 2, 4, NZ, 128), F32),
            pltpu.VMEM((STEPS, 2, 4, NZ, 128), F32),
            pltpu.VMEM((STEPS, 2, NZ, 128), F32),
            pltpu.VMEM((STEPS, 2, 2, NZ, 128), F32),
            pltpu.VMEM((2 * NZ, 128), F32),
            dma((1 + NK,)),
            dma((STEPS, 2, NK, 2)),
            dma((STEPS, 2, NK, 2)),
            dma((STEPS, 2, NK)),
            dma((STEPS, 2, NK)),
            dma((STEPS, 4, NK)),
            dma((STEPS, 4, NK)),
            dma,
            dma,
            dma((NK,)),
            dma((NK,)),
            dma((STEPS, 2)),
            dma((STEPS, 2)),
            dma((STEPS, 2)),
            dma((STEPS, 2)),
        ],
        compiler_params=pltpu.CompilerParams(
            collective_id=0, has_side_effects=True, vmem_limit_bytes=32 * 1024 * 1024
        ),
    )(x, land_mask, bottom_level, shortwave, absorb, reaction)
    return y.reshape(1, NF, NZ, 2, 128)


def solution(mesh):
    in_specs = (
        P("grp", None, None, "ty", "tx"),
        P("ty", "tx"),
        P("ty", "tx"),
        P("ty", "tx"),
        P(),
        P(),
    )
    out_specs = P("grp", None, None, "ty", "tx")
    return jax.shard_map(local, mesh=mesh, in_specs=in_specs, out_specs=out_specs, check_vma=False)
```

```python
import functools

import jax
import jax.numpy as jnp
from jax import lax
from jax.experimental import pallas as pl
from jax.experimental.pallas import tpu as pltpu
from jax.sharding import PartitionSpec as P

STEPS = 2
NF = 23
NT = 19
NZ = 32
CH = 8
NK = NZ // CH
MESH = pl.DeviceIdType.MESH
F32 = jnp.float32

integration_interval = 0.1
tracer_step = 0.08
coriolis = 0.8
barotropic_gradient_coefficient = 0.1
water_extinction = 0.04
layer_depth = 0.05
growth_peak = 2.0
half_light = 0.5
ratio_floor = 0.01

DIAGS = ((-1, -1), (-1, 1), (1, -1), (1, 1))


def lanes(shape):
    return lax.broadcasted_iota(jnp.int32, shape, len(shape) - 1)


def roll(x, shift):
    return pltpu.roll(x, shift % 128 if isinstance(shift, int) else shift, x.ndim - 1)


def cumulative(x):
    n = x.shape[0]
    level = lax.broadcasted_iota(jnp.int32, x.shape, 0)
    d = 1
    while d < n:
        x = x + jnp.where(level >= d, pltpu.roll(x, d, 0), 0.0)
        d *= 2
    return x


def inverse(x):
    r = pl.reciprocal(x, approx=True)
    return r * (2.0 - x * r)


def kernel(
    x, land_in, bottom_in, shortwave_in, absorb_in, reaction_in, out,
    V, H, PS, PT, PD, ADV, CO, ZC, ZS, D, DH, SS, ST, KD, land, bottom, shortwave, absorb, reaction,
    lsem, psem, row_s, row_r, col_s, col_r, diag_s, diag_r, dyn_s, dyn_r, tra_s, tra_r, ors, orr, ocs, ocr,
):
    grp, ty, tx = lax.axis_index("grp"), lax.axis_index("ty"), lax.axis_index("tx")
    nty, ntx = lax.axis_size("ty"), lax.axis_size("tx")
    has_y = (ty > 0, ty < nty - 1)
    has_x = (tx > 0, tx < ntx - 1)
    step_of = (-1, 1)

    def has_diag(i):
        a, b = DIAGS[i]
        return has_y[(a + 1) // 2] & has_x[(b + 1) // 2]

    barrier = pltpu.get_barrier_semaphore()
    count = jnp.int32(1)
    pl.semaphore_signal(barrier, inc=1, device_id={"grp": 1 - grp}, device_id_type=MESH)
    for d in range(2):
        count = count + has_y[d].astype(jnp.int32) + has_x[d].astype(jnp.int32)

        @pl.when(has_y[d])
        def _():
            pl.semaphore_signal(barrier, inc=1, device_id={"ty": ty + step_of[d]}, device_id_type=MESH)

        @pl.when(has_x[d])
        def _():
            pl.semaphore_signal(barrier, inc=1, device_id={"tx": tx + step_of[d]}, device_id_type=MESH)

    load = pltpu.make_async_copy(x, V.at[0], lsem.at[0])
    load.start()
    small = [
        pltpu.make_async_copy(source, to, psem.at[i])
        for i, (source, to) in enumerate(
            (
                (land_in, land),
                (bottom_in, bottom),
                (shortwave_in, shortwave),
                (absorb_in, absorb),
                (reaction_in, reaction),
            )
        )
    ]
    for copy in small:
        copy.start()

    def fill(ref, n):
        def body(i, c):
            ref[i] = jnp.zeros(ref.shape[1:], F32)
            return c

        lax.fori_loop(0, n, body, 0)

    lane8 = lanes((CH, 128))
    four8 = lane8 % 4
    first, last = lane8 == 0, lane8 == 127

    def tracer_side():
        n_diag = jnp.int32(0)
        for i in range(4):
            n_diag = n_diag + has_diag(i).astype(jnp.int32)

            @pl.when(has_diag(i))
            def _():
                a, b = DIAGS[i]
                pl.semaphore_signal(barrier, inc=1, device_id={"ty": ty + a, "tx": tx + b}, device_id_type=MESH)

            @pl.when(jnp.logical_not(has_diag(i)))
            def _():
                for s in range(STEPS):
                    PD[s, i] = jnp.zeros(PD.shape[2:], F32)

        for d in range(2):
            @pl.when(jnp.logical_not(has_y[d]))
            def _():
                for s in range(STEPS):
                    fill(H.at[s, d], NF)

            @pl.when(jnp.logical_not(has_x[d]))
            def _():
                for s in range(STEPS):
                    fill(PT.at[s, d], 2)

        def row_copy(s, d, k, part):
            lo, n = ((0, 2), (4, NT))[part]
            rows = pl.ds(pl.multiple_of(k * 16, 16), 16)
            src = (x if s == 0 else V.at[s]).at[pl.ds(lo, n), rows]
            return pltpu.make_async_remote_copy(
                src_ref=src,
                dst_ref=H.at[s, 1 - d, pl.ds(lo, n), rows],
                send_sem=row_s.at[s, d, k, part],
                recv_sem=row_r.at[s, 1 - d, k, part],
                device_id={"ty": ty + step_of[d]},
                device_id_type=MESH,
            )

        def row_arrival(s, d, k, part):
            lo, n = ((0, 2), (4, NT))[part]
            rows = pl.ds(pl.multiple_of(k * 16, 16), 16)
            return pltpu.make_async_remote_copy(
                src_ref=V.at[s, pl.ds(lo, n), rows],
                dst_ref=H.at[s, d, pl.ds(lo, n), rows],
                send_sem=row_s.at[s, d, k, part],
                recv_sem=row_r.at[s, d, k, part],
                device_id={"ty": ty + step_of[d]},
                device_id_type=MESH,
            )

        def col_copy(s, d, k, arrival=False):
            lev = pl.ds(pl.multiple_of(k * CH, CH), CH)
            to = d if arrival else 1 - d
            return pltpu.make_async_remote_copy(
                src_ref=PS.at[s, :, lev],
                dst_ref=PT.at[s, to, :, lev],
                send_sem=col_s.at[s, d, k],
                recv_sem=col_r.at[s, to, k],
                device_id={"tx": tx + step_of[d]},
                device_id_type=MESH,
            )

        def diag_copy(s, i, k, arrival=False):
            a, b = DIAGS[i]
            lev = pl.ds(pl.multiple_of(k * CH, CH), CH)
            to = i if arrival else 3 - i
            return pltpu.make_async_remote_copy(
                src_ref=PS.at[s, (a + 1) // 2, lev],
                dst_ref=PD.at[s, to, lev],
                send_sem=diag_s.at[s, i, k],
                recv_sem=diag_r.at[s, to, k],
                device_id={"ty": ty + a, "tx": tx + b},
                device_id_type=MESH,
            )

        def each_row(s, k, act):
            for d in range(2):
                @pl.when(has_y[d])
                def _():
                    for part in range(2):
                        act(s, d, k, part)

        def send_rows(s, k):
            each_row(s, k, lambda *a: row_copy(*a).start())

        def send_edges(s, k):
            for d in range(2):
                @pl.when(has_x[d])
                def _():
                    col_copy(s, d, k).start()
            for i in range(4):
                @pl.when(has_diag(i))
                def _():
                    diag_copy(s, i, k).start()

        def receive(s, k):
            for d in range(2):
                @pl.when(has_x[d])
                def _():
                    col_copy(s, d, k, True).wait_recv()
            for i in range(4):
                @pl.when(has_diag(i))
                def _():
                    diag_copy(s, i, k, True).wait_recv()
            each_row(s, k, lambda *a: row_arrival(*a).wait_recv())

        def sent(s, k):
            each_row(s, k, lambda *a: row_copy(*a).wait_send())
            for d in range(2):
                @pl.when(has_x[d])
                def _():
                    col_copy(s, d, k).wait_send()
            for i in range(4):
                @pl.when(has_diag(i))
                def _():
                    diag_copy(s, i, k).wait_send()

        def tracers_over(k):
            rows = pl.ds(pl.multiple_of(k * 16, 16), 16)
            return pltpu.make_async_remote_copy(
                src_ref=V.at[1, pl.ds(4, NT), rows],
                dst_ref=V.at[2, pl.ds(4, NT), rows],
                send_sem=tra_s.at[k],
                recv_sem=tra_r.at[k],
                device_id={"grp": 1 - grp},
                device_id_type=MESH,
            )

        def store_out(k):
            rows = pl.ds(pl.multiple_of(k * 16, 16), 16)
            return pltpu.make_async_copy(V.at[2, pl.ds(4, NT), rows], out.at[pl.ds(4, NT), rows], lsem.at[1 + k])

        def pack(s, start, count):
            lane = lanes((count, 128))
            quarter = lane // 4

            def body(f, rows):
                shift = 4 * f + 2
                return tuple(
                    jnp.where(quarter == f, roll(V[s, f, pl.ds(2 * start + r, count, 2), :], shift), rows[r])
                    for r in range(2)
                )

            zero = jnp.zeros((count, 128), F32)
            packed = lax.fori_loop(0, NF, body, (zero, zero), unroll=True)
            for r in range(2):
                PS[s, r, pl.ds(start, count), :] = packed[r]

        def chunk(s, k, carry):
            base = k * 16
            lev = pl.ds(pl.multiple_of(k * CH, CH), CH)

            def row(f, r):
                at = pl.ds(base + r % 2, CH, 2)
                if r < 0:
                    return H[s, 0, f, at, :]
                if r > 1:
                    return H[s, 1, f, at, :]
                return V[s, f, at, :]

            y_lo = jnp.where(has_y[0], 0.02, 0.0).astype(F32)
            y_hi = jnp.where(has_y[1], 0.02, 0.0).astype(F32)
            x_lo = jnp.where(has_x[0], 0.02, 0.0).astype(F32)
            x_hi = jnp.where(has_x[1], 0.02, 0.0).astype(F32)
            right = four8 == 1
            left = four8 == 2

            own = [PS[s, r, lev, :] for r in range(2)]
            low = [PD[s, 0, lev, :], PT[s, 0, 0, lev, :], PT[s, 0, 1, lev, :], PD[s, 2, lev, :]]
            high = [PD[s, 1, lev, :], PT[s, 1, 0, lev, :], PT[s, 1, 1, lev, :], PD[s, 3, lev, :]]
            mid = [jnp.where(right, roll(high[i], -1), roll(low[i], 1)) for i in range(4)]
            for i in range(4):
                ZC[i] = mid[i]
            north = [jnp.where(right, roll(high[1 + r], -2), own[r]) for r in range(2)]
            south = [jnp.where(right, own[r], roll(low[1 + r], 2)) for r in range(2)]

            def spread(value, f):
                value = jnp.where(lane8 // 4 == f, value, 0.0)
                for d in (4, 8, 16, 32, 64):
                    value = value + roll(value, d)
                return value

            def face(q, a, b):
                anti = jnp.abs(q) * (b - a)
                return anti, q * (a + b) - anti

            def bounds(centre, others):
                hi = lo = centre
                for o in others:
                    hi, lo = jnp.maximum(hi, o), jnp.minimum(lo, o)
                return hi, lo

            def gains(w, e, n, so):
                gain_in = (jnp.maximum(w, 0.0) - jnp.minimum(e, 0.0)) + (jnp.maximum(so, 0.0) - jnp.minimum(n, 0.0))
                gain_out = (jnp.maximum(e, 0.0) - jnp.minimum(w, 0.0)) + (jnp.maximum(n, 0.0) - jnp.minimum(so, 0.0))
                return gain_in, gain_out

            def ratio(gain, room):
                return jnp.minimum(gain, jnp.maximum(room, 0.0)) * inverse(
                    jnp.maximum(gain, ratio_floor * tracer_step)
                )

            u_mid = [spread(m, 0) for m in mid]
            q_rows = [
                (u_mid[0] + u_mid[1]) * y_lo,
                (u_mid[1] + u_mid[2]) * 0.02,
                (u_mid[2] + u_mid[3]) * y_hi,
            ]
            faces = [face(q_rows[i], mid[i], mid[i + 1]) for i in range(3)]
            for r in range(2):
                v_mid = spread(mid[1 + r], 1)
                q_n = (v_mid + spread(north[r], 1)) * jnp.where(left, x_lo, 0.02)
                q_s = (v_mid + spread(south[r], 1)) * jnp.where(right, x_hi, 0.02)
                a_n, l_n = face(q_n, mid[1 + r], north[r])
                a_s, l_s = face(q_s, south[r], mid[1 + r])
                a_w, l_w = faces[r]
                a_e, l_e = faces[r + 1]
                lowered = mid[1 + r] - (l_e - l_w + l_n - l_s)
                hi, lo = bounds(mid[1 + r], (mid[r], mid[2 + r], north[r], south[r]))
                gain_in, gain_out = gains(a_w, a_e, a_n, a_s)
                take_in = (right & (a_s >= 0.0)) | (jnp.logical_not(right) & (a_n < 0.0))
                gain = jnp.where(take_in, gain_in, gain_out)
                room = jnp.where(take_in, hi - lowered, lowered - lo)
                ZS[r] = ratio(gain, room)

            u = [row(0, r) for r in range(-2, 4)]
            for i, scale in enumerate((0.02, y_lo, 0.02, y_hi, 0.02)):
                CO[i] = (u[i] + u[i + 1]) * scale
            for i in range(4):
                v = row(1, i - 1)
                side = roll(mid[i], 126 - 4)
                CO[5 + i] = (v + jnp.where(last, side, roll(v, -1))) * jnp.where(last, x_hi, 0.02)
                CO[9 + i] = (v + jnp.where(first, side, roll(v, 1))) * jnp.where(first, x_lo, 0.02)

            def transport(t, extinction):
                f = t + 4
                c = [row(f, r) for r in range(-2, 4)]
                turn = 126 - 4 * f
                fe = [face(CO[i], c[i], c[i + 1]) for i in range(5)]
                lowered, ratio_in, ratio_out, an, as_ = {}, {}, {}, {}, {}
                for i in range(1, 5):
                    side = roll(ZC[i - 1], turn)
                    c_n = jnp.where(last, side, roll(c[i], -1))
                    c_s = jnp.where(first, side, roll(c[i], 1))
                    a_n, l_n = face(CO[4 + i], c[i], c_n)
                    a_s, l_s = face(CO[8 + i], c_s, c[i])
                    a_w, l_w = fe[i - 1]
                    a_e, l_e = fe[i]
                    low_c = c[i] - (l_e - l_w + l_n - l_s)
                    hi, lo = bounds(c[i], (c[i - 1], c[i + 1], c_n, c_s))
                    gain_in, gain_out = gains(a_w, a_e, a_n, a_s)
                    room_in, room_out = hi - low_c, low_c - lo
                    if i in (1, 4):
                        take_in = a_e < 0.0 if i == 1 else a_w >= 0.0
                        ratio_in[i] = ratio(
                            jnp.where(take_in, gain_in, gain_out), jnp.where(take_in, room_in, room_out)
                        )
                    else:
                        lowered[i], an[i], as_[i] = low_c, a_n, a_s
                        ratio_in[i] = ratio(gain_in, room_in)
                        ratio_out[i] = ratio(gain_out, room_out)
                a = fe[1][0]
                f_lo = a * jnp.minimum(ratio_in[1], jnp.where(a >= 0.0, ratio_in[2], ratio_out[2]))
                a = fe[2][0]
                f_mid = a * jnp.where(
                    a >= 0.0,
                    jnp.minimum(ratio_in[3], ratio_out[2]),
                    jnp.minimum(ratio_in[2], ratio_out[3]),
                )
                a = fe[3][0]
                f_hi = a * jnp.minimum(jnp.where(a >= 0.0, ratio_out[3], ratio_in[3]), ratio_in[4])
                result = []
                for i, f_w, f_e in ((2, f_lo, f_mid), (3, f_mid, f_hi)):
                    side = roll(ZS[i - 2], turn)
                    a_n, a_s = an[i], as_[i]
                    up = a_n >= 0.0
                    mine = jnp.where(up, ratio_out[i], ratio_in[i])
                    other = jnp.where(up, roll(ratio_in[i], -1), roll(ratio_out[i], -1))
                    f_n = a_n * jnp.minimum(mine, jnp.where(last, side, other))
                    at_rim = a_s * jnp.minimum(side, jnp.where(a_s >= 0.0, ratio_in[i], ratio_out[i]))
                    f_s = jnp.where(first, at_rim, roll(f_n, 1))
                    advected = lowered[i] - (f_e - f_w + f_n - f_s)
                    ADV[t, i - 2] = advected
                    result.append(extinction[i - 2] + absorb[t] * advected)
                return tuple(result)

            base_light = jnp.full((CH, 128), water_extinction, F32)
            extinction = lax.fori_loop(0, NT, transport, (base_light, base_light), unroll=True)

            level = k * CH + lax.broadcasted_iota(jnp.int32, (CH, 128), 0)
            wet, growth, carries = [], [], []
            for r in range(2):
                total = cumulative(extinction[r]) + carry[r]
                carries.append(carry[r] + jnp.sum(extinction[r], axis=0, keepdims=True))
                below = shortwave[pl.ds(r, 1), :] * jnp.exp(-layer_depth * total)
                sea = (land[pl.ds(r, 1), :] == 1) & (level < bottom[pl.ds(r, 1), :])
                wet.append(jnp.where(sea, 1.0, 0.0))
                grow = (
                    growth_peak
                    * jnp.exp(0.063 * row(2, r))
                    * below
                    / (below + half_light)
                    * (1.0 + 0.2 * jnp.tanh(row(3, r)))
                )
                growth.append(wet[r] * (tracer_step * grow))

            def react(o, c):
                for r in range(2):
                    mixed = reaction[o, 0] * ADV[0, r]
                    for t in range(1, NT):
                        mixed = mixed + reaction[o, t] * ADV[t, r]
                    V[s + 1, o + 4, pl.ds(base + r, CH, 2), :] = wet[r] * ADV[o, r] + growth[r] * mixed
                return c

            lax.fori_loop(0, NT, react, 0, unroll=True)
            return tuple(carries)

        dynamics_in = pltpu.make_async_remote_copy(
            src_ref=V.at[1, pl.ds(0, 4)],
            dst_ref=V.at[1, pl.ds(0, 4)],
            send_sem=dyn_s,
            recv_sem=dyn_r,
            device_id={"grp": 1 - grp},
            device_id_type=MESH,
        )
        dynamics_out = pltpu.make_async_copy(V.at[1, pl.ds(0, 4)], out.at[pl.ds(0, 4)], lsem.at[0])

        load.wait()
        for copy in small:
            copy.wait()
        pack(0, 0, NZ)
        pl.semaphore_wait(barrier, count + n_diag)

        def begin(k, c):
            send_rows(0, k)
            send_edges(0, k)
            return c

        lax.fori_loop(0, NK, begin, 0)

        zero = jnp.zeros((1, 128), F32)

        def first_step(k, carry):
            receive(0, k)
            carry = chunk(0, k, carry)

            @pl.when(k == 0)
            def _():
                dynamics_in.wait_recv()
                dynamics_out.start()

            send_rows(1, k)
            pack(1, k * CH, CH)
            send_edges(1, k)
            tracers_over(k).start()
            return carry

        lax.fori_loop(0, NK, first_step, (zero, zero))

        def second_step(k, carry):
            receive(1, k)
            carry = chunk(1, k, carry)
            store_out(k).start()
            return carry

        lax.fori_loop(0, NK, second_step, (zero, zero))

        def finish(k, c):
            sent(0, k)
            sent(1, k)
            tracers_over(k).wait_send()
            store_out(k).wait()
            return c

        lax.fori_loop(0, NK, finish, 0)
        dynamics_out.wait()

    def ocean_side():
        for d in range(2):
            @pl.when(jnp.logical_not(has_y[d]))
            def _():
                for s in range(STEPS):
                    fill(DH.at[s, d], 4)

            @pl.when(jnp.logical_not(has_x[d]))
            def _():
                for s in range(STEPS):
                    fill(ST.at[s, d], 2)

        lane = lanes((NZ, 128))
        four, quarter = lane % 4, lane // 4
        first_z, last_z = lane == 0, lane == 127

        def row_copy(s, d, arrival=False):
            to = d if arrival else 1 - d
            return pltpu.make_async_remote_copy(
                src_ref=D.at[s, d],
                dst_ref=DH.at[s, to],
                send_sem=ors.at[s, d],
                recv_sem=orr.at[s, to],
                device_id={"ty": ty + step_of[d]},
                device_id_type=MESH,
            )

        def col_copy(s, d, arrival=False):
            to = d if arrival else 1 - d
            return pltpu.make_async_remote_copy(
                src_ref=SS.at[s],
                dst_ref=ST.at[s, to],
                send_sem=ocs.at[s, d],
                recv_sem=ocr.at[s, to],
                device_id={"tx": tx + step_of[d]},
                device_id_type=MESH,
            )

        def exchange(s, act):
            for d in range(2):
                @pl.when(has_y[d])
                def _():
                    act(row_copy, s, d)

                @pl.when(has_x[d])
                def _():
                    act(col_copy, s, d)

        def pack(s):
            for r in range(2):
                packed = jnp.zeros((NZ, 128), F32)
                for f in range(4):
                    packed = jnp.where(quarter == f, roll(D[s, r, f], 4 * f + 2), packed)
                SS[s, r] = packed

        def light(ref):
            def body(t, acc):
                return acc + absorb[t] * ref[t + 4]

            KD[...] = lax.fori_loop(0, NT, body, jnp.full((2 * NZ, 128), water_extinction, F32))

        def update(s):
            level = lax.broadcasted_iota(jnp.int32, (NZ, 128), 0)
            for r in range(2):
                side = jnp.where(four == 1, roll(ST[s, 1, r], -1), roll(ST[s, 0, r], 1))
                own, lap, e_w, n_s = [], [], [], []
                for f in range(4):
                    c = D[s, r, f]
                    w = DH[s, 0, f] if r == 0 else D[s, 0, f]
                    e = DH[s, 1, f] if r == 1 else D[s, 1, f]
                    rim = roll(side, 126 - 4 * f)
                    n = jnp.where(last_z, rim, roll(c, -1))
                    so = jnp.where(first_z, rim, roll(c, 1))
                    own.append(c)
                    lap.append((e + w + n + so) - 4.0 * c)
                    e_w.append(e - w)
                    n_s.append(n - so)
                half = 0.5 * barotropic_gradient_coefficient
                grad_east = cumulative((-0.2 * e_w[2] + 0.8 * e_w[3]) * half)
                grad_north = cumulative((-0.2 * n_s[2] + 0.8 * n_s[3]) * half)
                extinction = KD[pl.ds(r, NZ, 2), :]
                below = shortwave[pl.ds(r, 1), :] * jnp.exp(-layer_depth * cumulative(extinction))
                above = below * jnp.exp(layer_depth * extinction)
                sea = (land[pl.ds(r, 1), :] == 1) & (level < bottom[pl.ds(r, 1), :])
                wet = jnp.where(sea, 1.0, 0.0)
                step = integration_interval
                new = (
                    own[0] + step * (coriolis * own[1] - grad_east + lap[0]),
                    own[1] + step * (-coriolis * own[0] - grad_north + lap[1]),
                    own[2] + step * (lap[2] + (above - below) / layer_depth),
                    own[3] + step * lap[3],
                )
                for f in range(4):
                    value = wet * new[f]
                    V[s + 1, f, pl.ds(r, NZ, 2), :] = value
                    if s + 1 < STEPS:
                        D[s + 1, r, f] = value

        dynamics_over = pltpu.make_async_remote_copy(
            src_ref=V.at[1, pl.ds(0, 4)],
            dst_ref=V.at[1, pl.ds(0, 4)],
            send_sem=dyn_s,
            recv_sem=dyn_r,
            device_id={"grp": 1 - grp},
            device_id_type=MESH,
        )

        def tracers_in(k):
            rows = pl.ds(pl.multiple_of(k * 16, 16), 16)
            return pltpu.make_async_remote_copy(
                src_ref=V.at[1, pl.ds(4, NT), rows],
                dst_ref=V.at[2, pl.ds(4, NT), rows],
                send_sem=tra_s.at[k],
                recv_sem=tra_r.at[k],
                device_id={"grp": 1 - grp},
                device_id_type=MESH,
            )

        load.wait()
        for copy in small:
            copy.wait()
        for r in range(2):
            for f in range(4):
                D[0, r, f] = V[0, f, pl.ds(r, NZ, 2), :]
        pack(0)
        pl.semaphore_wait(barrier, count)
        exchange(0, lambda copy, s, d: copy(s, d).start())
        light(V.at[0])
        exchange(0, lambda copy, s, d: copy(s, d, True).wait_recv())
        update(0)
        dynamics_over.start()
        pack(1)
        exchange(1, lambda copy, s, d: copy(s, d).start())

        def tracers_out(k):
            rows = pl.ds(pl.multiple_of(k * 16, 16), 16)
            return pltpu.make_async_copy(V.at[2, pl.ds(4, NT), rows], out.at[pl.ds(4, NT), rows], lsem.at[1 + k])

        def arrive(k, c):
            tracers_in(k).wait_recv()
            tracers_out(k).start()
            return c

        lax.fori_loop(0, NK, arrive, 0)
        light(V.at[2])
        exchange(1, lambda copy, s, d: copy(s, d, True).wait_recv())
        update(1)
        dynamics_out = pltpu.make_async_copy(V.at[2, pl.ds(0, 4)], out.at[pl.ds(0, 4)], lsem.at[0])
        dynamics_out.start()
        exchange(0, lambda copy, s, d: copy(s, d).wait_send())
        exchange(1, lambda copy, s, d: copy(s, d).wait_send())
        dynamics_over.wait_send()

        def finish(k, c):
            tracers_out(k).wait()
            return c

        lax.fori_loop(0, NK, finish, 0)
        dynamics_out.wait()

    pl.when(grp == 1)(tracer_side)
    pl.when(grp == 0)(ocean_side)


def local(coupled_state, land_mask, bottom_level, shortwave, absorb, reaction):
    x = coupled_state.reshape(NF, 2 * NZ, 128)
    hbm = pl.BlockSpec(memory_space=pltpu.HBM)
    dma = pltpu.SemaphoreType.DMA
    y = pl.pallas_call(
        kernel,
        out_shape=jax.ShapeDtypeStruct((NF, 2 * NZ, 128), F32),
        in_specs=[hbm] * 6,
        out_specs=hbm,
        scratch_shapes=[
            pltpu.VMEM((STEPS + 1, NF, 2 * NZ, 128), F32),
            pltpu.VMEM((STEPS, 2, NF, 2 * NZ, 128), F32),
            pltpu.VMEM((STEPS, 2, NZ, 128), F32),
            pltpu.VMEM((STEPS, 2, 2, NZ, 128), F32),
            pltpu.VMEM((STEPS, 4, NZ, 128), F32),
            pltpu.VMEM((NT, 2, CH, 128), F32),
            pltpu.VMEM((13, CH, 128), F32),
            pltpu.VMEM((4, CH, 128), F32),
            pltpu.VMEM((2, CH, 128), F32),
            pltpu.VMEM((STEPS, 2, 4, NZ, 128), F32),
            pltpu.VMEM((STEPS, 2, 4, NZ, 128), F32),
            pltpu.VMEM((STEPS, 2, NZ, 128), F32),
            pltpu.VMEM((STEPS, 2, 2, NZ, 128), F32),
            pltpu.VMEM((2 * NZ, 128), F32),
            pltpu.VMEM((2, 128), jnp.int32),
            pltpu.VMEM((2, 128), jnp.int32),
            pltpu.VMEM((2, 128), F32),
            pltpu.SMEM((NT,), F32),
            pltpu.SMEM((NT, NT), F32),
            dma((1 + NK,)),
            dma((5,)),
            dma((STEPS, 2, NK, 2)),
            dma((STEPS, 2, NK, 2)),
            dma((STEPS, 2, NK)),
            dma((STEPS, 2, NK)),
            dma((STEPS, 4, NK)),
            dma((STEPS, 4, NK)),
            dma,
            dma,
            dma((NK,)),
            dma((NK,)),
            dma((STEPS, 2)),
            dma((STEPS, 2)),
            dma((STEPS, 2)),
            dma((STEPS, 2)),
        ],
        compiler_params=pltpu.CompilerParams(
            collective_id=0, has_side_effects=True
        ),
    )(x, land_mask, bottom_level, shortwave, absorb, reaction)
    return y.reshape(1, NF, NZ, 2, 128)


def solution(mesh):
    in_specs = (
        P("grp", None, None, "ty", "tx"),
        P("ty", "tx"),
        P("ty", "tx"),
        P("ty", "tx"),
        P(),
        P(),
    )
    out_specs = P("grp", None, None, "ty", "tx")
    return jax.shard_map(local, mesh=mesh, in_specs=in_specs, out_specs=out_specs, check_vma=False)
```

```python
import functools

import jax
import jax.numpy as jnp
from jax import lax
from jax.experimental import pallas as pl
from jax.experimental.pallas import tpu as pltpu
from jax.sharding import PartitionSpec as P

STEPS = 2
NF = 23
NT = 19
NZ = 32
CH = 8
NK = NZ // CH
MESH = pl.DeviceIdType.MESH
F32 = jnp.float32

integration_interval = 0.1
tracer_step = 0.08
coriolis = 0.8
barotropic_gradient_coefficient = 0.1
water_extinction = 0.04
layer_depth = 0.05
growth_peak = 2.0
half_light = 0.5
ratio_floor = 0.01

DIAGS = ((-1, -1), (-1, 1), (1, -1), (1, 1))


def lanes(shape):
    return lax.broadcasted_iota(jnp.int32, shape, len(shape) - 1)


def roll(x, shift):
    return pltpu.roll(x, shift % 128 if isinstance(shift, int) else shift, x.ndim - 1)


def cumulative(x):
    n = x.shape[0]
    level = lax.broadcasted_iota(jnp.int32, x.shape, 0)
    d = 1
    while d < n:
        x = x + jnp.where(level >= d, pltpu.roll(x, d, 0), 0.0)
        d *= 2
    return x


def inverse(x):
    r = pl.reciprocal(x, approx=True)
    return r * (2.0 - x * r)


def kernel(
    x, land_in, bottom_in, shortwave_in, absorb_in, reaction_in, out,
    V, H, PS, PT, PD, ADV, CO, ZC, ZS, D, DH, SS, ST, KD, land, bottom, shortwave, absorb, reaction,
    lsem, psem, row_s, row_r, col_s, col_r, diag_s, diag_r, dyn_s, dyn_r, tra_s, tra_r, ors, orr, ocs, ocr,
):
    grp, ty, tx = lax.axis_index("grp"), lax.axis_index("ty"), lax.axis_index("tx")
    nty, ntx = lax.axis_size("ty"), lax.axis_size("tx")
    has_y = (ty > 0, ty < nty - 1)
    has_x = (tx > 0, tx < ntx - 1)
    step_of = (-1, 1)

    def has_diag(i):
        a, b = DIAGS[i]
        return has_y[(a + 1) // 2] & has_x[(b + 1) // 2]

    barrier = pltpu.get_barrier_semaphore()
    count = jnp.int32(1)
    pl.semaphore_signal(barrier, inc=1, device_id={"grp": 1 - grp}, device_id_type=MESH)
    for d in range(2):
        count = count + has_y[d].astype(jnp.int32) + has_x[d].astype(jnp.int32)

        @pl.when(has_y[d])
        def _():
            pl.semaphore_signal(barrier, inc=1, device_id={"ty": ty + step_of[d]}, device_id_type=MESH)

        @pl.when(has_x[d])
        def _():
            pl.semaphore_signal(barrier, inc=1, device_id={"tx": tx + step_of[d]}, device_id_type=MESH)

    load = pltpu.make_async_copy(x, V.at[0], lsem.at[0])
    load.start()
    small = [
        pltpu.make_async_copy(source, to, psem.at[i])
        for i, (source, to) in enumerate(
            (
                (land_in, land),
                (bottom_in, bottom),
                (shortwave_in, shortwave),
                (absorb_in, absorb),
                (reaction_in, reaction),
            )
        )
    ]
    for copy in small:
        copy.start()

    def fill(ref, n):
        def body(i, c):
            ref[i] = jnp.zeros(ref.shape[1:], F32)
            return c

        lax.fori_loop(0, n, body, 0)

    lane8 = lanes((CH, 128))
    four8 = lane8 % 4
    first, last = lane8 == 0, lane8 == 127

    def tracer_side():
        n_diag = jnp.int32(0)
        for i in range(4):
            n_diag = n_diag + has_diag(i).astype(jnp.int32)

            @pl.when(has_diag(i))
            def _():
                a, b = DIAGS[i]
                pl.semaphore_signal(barrier, inc=1, device_id={"ty": ty + a, "tx": tx + b}, device_id_type=MESH)

            @pl.when(jnp.logical_not(has_diag(i)))
            def _():
                for s in range(STEPS):
                    PD[s, i] = jnp.zeros(PD.shape[2:], F32)

        for d in range(2):
            @pl.when(jnp.logical_not(has_y[d]))
            def _():
                for s in range(STEPS):
                    fill(H.at[s, d], NF)

            @pl.when(jnp.logical_not(has_x[d]))
            def _():
                for s in range(STEPS):
                    fill(PT.at[s, d], 2)

        def row_copy(s, d, k, part):
            lo, n = ((0, 2), (4, NT))[part]
            rows = pl.ds(pl.multiple_of(k * 16, 16), 16)
            src = (x if s == 0 else V.at[s]).at[pl.ds(lo, n), rows]
            return pltpu.make_async_remote_copy(
                src_ref=src,
                dst_ref=H.at[s, 1 - d, pl.ds(lo, n), rows],
                send_sem=row_s.at[s, d, k, part],
                recv_sem=row_r.at[s, 1 - d, k, part],
                device_id={"ty": ty + step_of[d]},
                device_id_type=MESH,
            )

        def row_arrival(s, d, k, part):
            lo, n = ((0, 2), (4, NT))[part]
            rows = pl.ds(pl.multiple_of(k * 16, 16), 16)
            return pltpu.make_async_remote_copy(
                src_ref=V.at[s, pl.ds(lo, n), rows],
                dst_ref=H.at[s, d, pl.ds(lo, n), rows],
                send_sem=row_s.at[s, d, k, part],
                recv_sem=row_r.at[s, d, k, part],
                device_id={"ty": ty + step_of[d]},
                device_id_type=MESH,
            )

        def col_copy(s, d, k, arrival=False):
            lev = pl.ds(pl.multiple_of(k * CH, CH), CH)
            to = d if arrival else 1 - d
            return pltpu.make_async_remote_copy(
                src_ref=PS.at[s, :, lev],
                dst_ref=PT.at[s, to, :, lev],
                send_sem=col_s.at[s, d, k],
                recv_sem=col_r.at[s, to, k],
                device_id={"tx": tx + step_of[d]},
                device_id_type=MESH,
            )

        def diag_copy(s, i, k, arrival=False):
            a, b = DIAGS[i]
            lev = pl.ds(pl.multiple_of(k * CH, CH), CH)
            to = i if arrival else 3 - i
            return pltpu.make_async_remote_copy(
                src_ref=PS.at[s, (a + 1) // 2, lev],
                dst_ref=PD.at[s, to, lev],
                send_sem=diag_s.at[s, i, k],
                recv_sem=diag_r.at[s, to, k],
                device_id={"ty": ty + a, "tx": tx + b},
                device_id_type=MESH,
            )

        def each_row(s, k, act):
            for d in range(2):
                @pl.when(has_y[d])
                def _():
                    for part in range(2):
                        act(s, d, k, part)

        def send_rows(s, k):
            each_row(s, k, lambda *a: row_copy(*a).start())

        def send_edges(s, k):
            for d in range(2):
                @pl.when(has_x[d])
                def _():
                    col_copy(s, d, k).start()
            for i in range(4):
                @pl.when(has_diag(i))
                def _():
                    diag_copy(s, i, k).start()

        def receive(s, k):
            for d in range(2):
                @pl.when(has_x[d])
                def _():
                    col_copy(s, d, k, True).wait_recv()
            for i in range(4):
                @pl.when(has_diag(i))
                def _():
                    diag_copy(s, i, k, True).wait_recv()
            each_row(s, k, lambda *a: row_arrival(*a).wait_recv())

        def sent(s, k):
            each_row(s, k, lambda *a: row_copy(*a).wait_send())
            for d in range(2):
                @pl.when(has_x[d])
                def _():
                    col_copy(s, d, k).wait_send()
            for i in range(4):
                @pl.when(has_diag(i))
                def _():
                    diag_copy(s, i, k).wait_send()

        def tracers_over(k):
            rows = pl.ds(pl.multiple_of(k * 16, 16), 16)
            return pltpu.make_async_remote_copy(
                src_ref=V.at[1, pl.ds(4, NT), rows],
                dst_ref=V.at[2, pl.ds(4, NT), rows],
                send_sem=tra_s.at[k],
                recv_sem=tra_r.at[k],
                device_id={"grp": 1 - grp},
                device_id_type=MESH,
            )

        def store_out(k):
            rows = pl.ds(pl.multiple_of(k * 16, 16), 16)
            return pltpu.make_async_copy(V.at[2, pl.ds(4, NT), rows], out.at[pl.ds(4, NT), rows], lsem.at[1 + k])

        def pack(s, start, count):
            lane = lanes((count, 128))
            quarter = lane // 4

            def body(f, rows):
                shift = 4 * f + 2
                return tuple(
                    jnp.where(quarter == f, roll(V[s, f, pl.ds(2 * start + r, count, 2), :], shift), rows[r])
                    for r in range(2)
                )

            zero = jnp.zeros((count, 128), F32)
            packed = lax.fori_loop(0, NF, body, (zero, zero), unroll=True)
            for r in range(2):
                PS[s, r, pl.ds(start, count), :] = packed[r]

        def chunk(s, k, carry):
            base = k * 16
            lev = pl.ds(pl.multiple_of(k * CH, CH), CH)

            def row(f, r):
                at = pl.ds(base + r % 2, CH, 2)
                if r < 0:
                    return H[s, 0, f, at, :]
                if r > 1:
                    return H[s, 1, f, at, :]
                return V[s, f, at, :]

            y_lo = jnp.where(has_y[0], 0.02, 0.0).astype(F32)
            y_hi = jnp.where(has_y[1], 0.02, 0.0).astype(F32)
            x_lo = jnp.where(has_x[0], 0.02, 0.0).astype(F32)
            x_hi = jnp.where(has_x[1], 0.02, 0.0).astype(F32)
            right = four8 == 1
            left = four8 == 2

            own = [PS[s, r, lev, :] for r in range(2)]
            low = [PD[s, 0, lev, :], PT[s, 0, 0, lev, :], PT[s, 0, 1, lev, :], PD[s, 2, lev, :]]
            high = [PD[s, 1, lev, :], PT[s, 1, 0, lev, :], PT[s, 1, 1, lev, :], PD[s, 3, lev, :]]
            mid = [jnp.where(right, roll(high[i], -1), roll(low[i], 1)) for i in range(4)]
            for i in range(4):
                ZC[i] = mid[i]
            north = [jnp.where(right, roll(high[1 + r], -2), own[r]) for r in range(2)]
            south = [jnp.where(right, own[r], roll(low[1 + r], 2)) for r in range(2)]

            def spread(value, f):
                value = jnp.where(lane8 // 4 == f, value, 0.0)
                for d in (4, 8, 16, 32, 64):
                    value = value + roll(value, d)
                return value

            def face(q, a, b):
                anti = jnp.abs(q) * (b - a)
                return anti, q * (a + b) - anti

            def bounds(centre, others):
                hi = lo = centre
                for o in others:
                    hi, lo = jnp.maximum(hi, o), jnp.minimum(lo, o)
                return hi, lo

            def gains(w, e, n, so):
                gain_in = (jnp.maximum(w, 0.0) - jnp.minimum(e, 0.0)) + (jnp.maximum(so, 0.0) - jnp.minimum(n, 0.0))
                gain_out = (jnp.maximum(e, 0.0) - jnp.minimum(w, 0.0)) + (jnp.maximum(n, 0.0) - jnp.minimum(so, 0.0))
                return gain_in, gain_out

            def ratio(gain, room):
                return jnp.minimum(gain, jnp.maximum(room, 0.0)) * inverse(
                    jnp.maximum(gain, ratio_floor * tracer_step)
                )

            u_mid = [spread(m, 0) for m in mid]
            q_rows = [
                (u_mid[0] + u_mid[1]) * y_lo,
                (u_mid[1] + u_mid[2]) * 0.02,
                (u_mid[2] + u_mid[3]) * y_hi,
            ]
            faces = [face(q_rows[i], mid[i], mid[i + 1]) for i in range(3)]
            for r in range(2):
                v_mid = spread(mid[1 + r], 1)
                q_n = (v_mid + spread(north[r], 1)) * jnp.where(left, x_lo, 0.02)
                q_s = (v_mid + spread(south[r], 1)) * jnp.where(right, x_hi, 0.02)
                a_n, l_n = face(q_n, mid[1 + r], north[r])
                a_s, l_s = face(q_s, south[r], mid[1 + r])
                a_w, l_w = faces[r]
                a_e, l_e = faces[r + 1]
                lowered = mid[1 + r] - (l_e - l_w + l_n - l_s)
                hi, lo = bounds(mid[1 + r], (mid[r], mid[2 + r], north[r], south[r]))
                gain_in, gain_out = gains(a_w, a_e, a_n, a_s)
                take_in = (right & (a_s >= 0.0)) | (jnp.logical_not(right) & (a_n < 0.0))
                gain = jnp.where(take_in, gain_in, gain_out)
                room = jnp.where(take_in, hi - lowered, lowered - lo)
                ZS[r] = ratio(gain, room)

            u = [row(0, r) for r in range(-2, 4)]
            for i, scale in enumerate((0.02, y_lo, 0.02, y_hi, 0.02)):
                CO[i] = (u[i] + u[i + 1]) * scale
            for i in range(4):
                v = row(1, i - 1)
                side = roll(mid[i], 126 - 4)
                CO[5 + i] = (v + jnp.where(last, side, roll(v, -1))) * jnp.where(last, x_hi, 0.02)
                CO[9 + i] = (v + jnp.where(first, side, roll(v, 1))) * jnp.where(first, x_lo, 0.02)

            def transport(t, extinction):
                f = t + 4
                c = [row(f, r) for r in range(-2, 4)]
                turn = 126 - 4 * f
                fe = [face(CO[i], c[i], c[i + 1]) for i in range(5)]
                lowered, ratio_in, ratio_out, an, as_ = {}, {}, {}, {}, {}
                for i in range(1, 5):
                    side = roll(ZC[i - 1], turn)
                    c_n = jnp.where(last, side, roll(c[i], -1))
                    c_s = jnp.where(first, side, roll(c[i], 1))
                    a_n, l_n = face(CO[4 + i], c[i], c_n)
                    a_s, l_s = face(CO[8 + i], c_s, c[i])
                    a_w, l_w = fe[i - 1]
                    a_e, l_e = fe[i]
                    low_c = c[i] - (l_e - l_w + l_n - l_s)
                    hi, lo = bounds(c[i], (c[i - 1], c[i + 1], c_n, c_s))
                    gain_in, gain_out = gains(a_w, a_e, a_n, a_s)
                    room_in, room_out = hi - low_c, low_c - lo
                    if i in (1, 4):
                        take_in = a_e < 0.0 if i == 1 else a_w >= 0.0
                        ratio_in[i] = ratio(
                            jnp.where(take_in, gain_in, gain_out), jnp.where(take_in, room_in, room_out)
                        )
                    else:
                        lowered[i], an[i], as_[i] = low_c, a_n, a_s
                        ratio_in[i] = ratio(gain_in, room_in)
                        ratio_out[i] = ratio(gain_out, room_out)
                a = fe[1][0]
                f_lo = a * jnp.minimum(ratio_in[1], jnp.where(a >= 0.0, ratio_in[2], ratio_out[2]))
                a = fe[2][0]
                f_mid = a * jnp.where(
                    a >= 0.0,
                    jnp.minimum(ratio_in[3], ratio_out[2]),
                    jnp.minimum(ratio_in[2], ratio_out[3]),
                )
                a = fe[3][0]
                f_hi = a * jnp.minimum(jnp.where(a >= 0.0, ratio_out[3], ratio_in[3]), ratio_in[4])
                result = []
                for i, f_w, f_e in ((2, f_lo, f_mid), (3, f_mid, f_hi)):
                    side = roll(ZS[i - 2], turn)
                    a_n, a_s = an[i], as_[i]
                    up = a_n >= 0.0
                    mine = jnp.where(up, ratio_out[i], ratio_in[i])
                    other = jnp.where(up, roll(ratio_in[i], -1), roll(ratio_out[i], -1))
                    f_n = a_n * jnp.minimum(mine, jnp.where(last, side, other))
                    at_rim = a_s * jnp.minimum(side, jnp.where(a_s >= 0.0, ratio_in[i], ratio_out[i]))
                    f_s = jnp.where(first, at_rim, roll(f_n, 1))
                    advected = lowered[i] - (f_e - f_w + f_n - f_s)
                    ADV[t, i - 2] = advected
                    result.append(extinction[i - 2] + absorb[t] * advected)
                return tuple(result)

            base_light = jnp.full((CH, 128), water_extinction, F32)
            extinction = lax.fori_loop(0, NT, transport, (base_light, base_light), unroll=True)

            level = k * CH + lax.broadcasted_iota(jnp.int32, (CH, 128), 0)
            wet, growth, carries = [], [], []
            for r in range(2):
                total = cumulative(extinction[r]) + carry[r]
                carries.append(carry[r] + jnp.sum(extinction[r], axis=0, keepdims=True))
                below = shortwave[pl.ds(r, 1), :] * jnp.exp(-layer_depth * total)
                sea = (land[pl.ds(r, 1), :] == 1) & (level < bottom[pl.ds(r, 1), :])
                wet.append(jnp.where(sea, 1.0, 0.0))
                grow = (
                    growth_peak
                    * jnp.exp(0.063 * row(2, r))
                    * below
                    / (below + half_light)
                    * (1.0 + 0.2 * jnp.tanh(row(3, r)))
                )
                growth.append(wet[r] * (tracer_step * grow))

            def react(o, c):
                for r in range(2):
                    mixed = reaction[o, 0] * ADV[0, r]
                    for t in range(1, NT):
                        mixed = mixed + reaction[o, t] * ADV[t, r]
                    V[s + 1, o + 4, pl.ds(base + r, CH, 2), :] = wet[r] * ADV[o, r] + growth[r] * mixed
                return c

            lax.fori_loop(0, NT, react, 0, unroll=True)
            return tuple(carries)

        dynamics_in = pltpu.make_async_remote_copy(
            src_ref=V.at[1, pl.ds(0, 4)],
            dst_ref=V.at[1, pl.ds(0, 4)],
            send_sem=dyn_s,
            recv_sem=dyn_r,
            device_id={"grp": 1 - grp},
            device_id_type=MESH,
        )
        dynamics_out = pltpu.make_async_copy(V.at[1, pl.ds(0, 4)], out.at[pl.ds(0, 4)], lsem.at[0])

        load.wait()
        for copy in small:
            copy.wait()
        pack(0, 0, NZ)
        pl.semaphore_wait(barrier, count + n_diag)

        def begin(k, c):
            send_edges(0, k)
            return c

        lax.fori_loop(0, NK, begin, 0)
        lax.fori_loop(0, NK, lambda k, c: (send_rows(0, k), c)[1], 0)

        zero = jnp.zeros((1, 128), F32)

        def first_step(k, carry):
            receive(0, k)
            carry = chunk(0, k, carry)

            @pl.when(k == 0)
            def _():
                dynamics_in.wait_recv()
                dynamics_out.start()

            pack(1, k * CH, CH)
            send_edges(1, k)
            send_rows(1, k)
            tracers_over(k).start()
            return carry

        lax.fori_loop(0, NK, first_step, (zero, zero))

        def second_step(k, carry):
            receive(1, k)
            carry = chunk(1, k, carry)
            store_out(k).start()
            return carry

        lax.fori_loop(0, NK, second_step, (zero, zero))

        def finish(k, c):
            sent(0, k)
            sent(1, k)
            tracers_over(k).wait_send()
            store_out(k).wait()
            return c

        lax.fori_loop(0, NK, finish, 0)
        dynamics_out.wait()

    def ocean_side():
        for d in range(2):
            @pl.when(jnp.logical_not(has_y[d]))
            def _():
                for s in range(STEPS):
                    fill(DH.at[s, d], 4)

            @pl.when(jnp.logical_not(has_x[d]))
            def _():
                for s in range(STEPS):
                    fill(ST.at[s, d], 2)

        lane = lanes((NZ, 128))
        four, quarter = lane % 4, lane // 4
        first_z, last_z = lane == 0, lane == 127

        def row_copy(s, d, arrival=False):
            to = d if arrival else 1 - d
            return pltpu.make_async_remote_copy(
                src_ref=D.at[s, d],
                dst_ref=DH.at[s, to],
                send_sem=ors.at[s, d],
                recv_sem=orr.at[s, to],
                device_id={"ty": ty + step_of[d]},
                device_id_type=MESH,
            )

        def col_copy(s, d, arrival=False):
            to = d if arrival else 1 - d
            return pltpu.make_async_remote_copy(
                src_ref=SS.at[s],
                dst_ref=ST.at[s, to],
                send_sem=ocs.at[s, d],
                recv_sem=ocr.at[s, to],
                device_id={"tx": tx + step_of[d]},
                device_id_type=MESH,
            )

        def exchange(s, act):
            for d in range(2):
                @pl.when(has_y[d])
                def _():
                    act(row_copy, s, d)

                @pl.when(has_x[d])
                def _():
                    act(col_copy, s, d)

        def pack(s):
            for r in range(2):
                packed = jnp.zeros((NZ, 128), F32)
                for f in range(4):
                    packed = jnp.where(quarter == f, roll(D[s, r, f], 4 * f + 2), packed)
                SS[s, r] = packed

        def light(ref):
            def body(t, acc):
                return acc + absorb[t] * ref[t + 4]

            KD[...] = lax.fori_loop(0, NT, body, jnp.full((2 * NZ, 128), water_extinction, F32))

        def update(s):
            level = lax.broadcasted_iota(jnp.int32, (NZ, 128), 0)
            for r in range(2):
                side = jnp.where(four == 1, roll(ST[s, 1, r], -1), roll(ST[s, 0, r], 1))
                own, lap, e_w, n_s = [], [], [], []
                for f in range(4):
                    c = D[s, r, f]
                    w = DH[s, 0, f] if r == 0 else D[s, 0, f]
                    e = DH[s, 1, f] if r == 1 else D[s, 1, f]
                    rim = roll(side, 126 - 4 * f)
                    n = jnp.where(last_z, rim, roll(c, -1))
                    so = jnp.where(first_z, rim, roll(c, 1))
                    own.append(c)
                    lap.append((e + w + n + so) - 4.0 * c)
                    e_w.append(e - w)
                    n_s.append(n - so)
                half = 0.5 * barotropic_gradient_coefficient
                grad_east = cumulative((-0.2 * e_w[2] + 0.8 * e_w[3]) * half)
                grad_north = cumulative((-0.2 * n_s[2] + 0.8 * n_s[3]) * half)
                extinction = KD[pl.ds(r, NZ, 2), :]
                below = shortwave[pl.ds(r, 1), :] * jnp.exp(-layer_depth * cumulative(extinction))
                above = below * jnp.exp(layer_depth * extinction)
                sea = (land[pl.ds(r, 1), :] == 1) & (level < bottom[pl.ds(r, 1), :])
                wet = jnp.where(sea, 1.0, 0.0)
                step = integration_interval
                new = (
                    own[0] + step * (coriolis * own[1] - grad_east + lap[0]),
                    own[1] + step * (-coriolis * own[0] - grad_north + lap[1]),
                    own[2] + step * (lap[2] + (above - below) / layer_depth),
                    own[3] + step * lap[3],
                )
                for f in range(4):
                    value = wet * new[f]
                    V[s + 1, f, pl.ds(r, NZ, 2), :] = value
                    if s + 1 < STEPS:
                        D[s + 1, r, f] = value

        dynamics_over = pltpu.make_async_remote_copy(
            src_ref=V.at[1, pl.ds(0, 4)],
            dst_ref=V.at[1, pl.ds(0, 4)],
            send_sem=dyn_s,
            recv_sem=dyn_r,
            device_id={"grp": 1 - grp},
            device_id_type=MESH,
        )

        def tracers_in(k):
            rows = pl.ds(pl.multiple_of(k * 16, 16), 16)
            return pltpu.make_async_remote_copy(
                src_ref=V.at[1, pl.ds(4, NT), rows],
                dst_ref=V.at[2, pl.ds(4, NT), rows],
                send_sem=tra_s.at[k],
                recv_sem=tra_r.at[k],
                device_id={"grp": 1 - grp},
                device_id_type=MESH,
            )

        load.wait()
        for copy in small:
            copy.wait()
        for r in range(2):
            for f in range(4):
                D[0, r, f] = V[0, f, pl.ds(r, NZ, 2), :]
        pack(0)
        pl.semaphore_wait(barrier, count)
        exchange(0, lambda copy, s, d: copy(s, d).start())
        light(V.at[0])
        exchange(0, lambda copy, s, d: copy(s, d, True).wait_recv())
        update(0)
        dynamics_over.start()
        pack(1)
        exchange(1, lambda copy, s, d: copy(s, d).start())

        def tracers_out(k):
            rows = pl.ds(pl.multiple_of(k * 16, 16), 16)
            return pltpu.make_async_copy(V.at[2, pl.ds(4, NT), rows], out.at[pl.ds(4, NT), rows], lsem.at[1 + k])

        def arrive(k, c):
            tracers_in(k).wait_recv()
            tracers_out(k).start()
            return c

        lax.fori_loop(0, NK, arrive, 0)
        light(V.at[2])
        exchange(1, lambda copy, s, d: copy(s, d, True).wait_recv())
        update(1)
        dynamics_out = pltpu.make_async_copy(V.at[2, pl.ds(0, 4)], out.at[pl.ds(0, 4)], lsem.at[0])
        dynamics_out.start()
        exchange(0, lambda copy, s, d: copy(s, d).wait_send())
        exchange(1, lambda copy, s, d: copy(s, d).wait_send())
        dynamics_over.wait_send()

        def finish(k, c):
            tracers_out(k).wait()
            return c

        lax.fori_loop(0, NK, finish, 0)
        dynamics_out.wait()

    pl.when(grp == 1)(tracer_side)
    pl.when(grp == 0)(ocean_side)


def local(coupled_state, land_mask, bottom_level, shortwave, absorb, reaction):
    x = coupled_state.reshape(NF, 2 * NZ, 128)
    hbm = pl.BlockSpec(memory_space=pltpu.HBM)
    dma = pltpu.SemaphoreType.DMA
    y = pl.pallas_call(
        kernel,
        out_shape=jax.ShapeDtypeStruct((NF, 2 * NZ, 128), F32),
        in_specs=[hbm] * 6,
        out_specs=hbm,
        scratch_shapes=[
            pltpu.VMEM((STEPS + 1, NF, 2 * NZ, 128), F32),
            pltpu.VMEM((STEPS, 2, NF, 2 * NZ, 128), F32),
            pltpu.VMEM((STEPS, 2, NZ, 128), F32),
            pltpu.VMEM((STEPS, 2, 2, NZ, 128), F32),
            pltpu.VMEM((STEPS, 4, NZ, 128), F32),
            pltpu.VMEM((NT, 2, CH, 128), F32),
            pltpu.VMEM((13, CH, 128), F32),
            pltpu.VMEM((4, CH, 128), F32),
            pltpu.VMEM((2, CH, 128), F32),
            pltpu.VMEM((STEPS, 2, 4, NZ, 128), F32),
            pltpu.VMEM((STEPS, 2, 4, NZ, 128), F32),
            pltpu.VMEM((STEPS, 2, NZ, 128), F32),
            pltpu.VMEM((STEPS, 2, 2, NZ, 128), F32),
            pltpu.VMEM((2 * NZ, 128), F32),
            pltpu.VMEM((2, 128), jnp.int32),
            pltpu.VMEM((2, 128), jnp.int32),
            pltpu.VMEM((2, 128), F32),
            pltpu.SMEM((NT,), F32),
            pltpu.SMEM((NT, NT), F32),
            dma((1 + NK,)),
            dma((5,)),
            dma((STEPS, 2, NK, 2)),
            dma((STEPS, 2, NK, 2)),
            dma((STEPS, 2, NK)),
            dma((STEPS, 2, NK)),
            dma((STEPS, 4, NK)),
            dma((STEPS, 4, NK)),
            dma,
            dma,
            dma((NK,)),
            dma((NK,)),
            dma((STEPS, 2)),
            dma((STEPS, 2)),
            dma((STEPS, 2)),
            dma((STEPS, 2)),
        ],
        compiler_params=pltpu.CompilerParams(
            collective_id=0, has_side_effects=True
        ),
    )(x, land_mask, bottom_level, shortwave, absorb, reaction)
    return y.reshape(1, NF, NZ, 2, 128)


def solution(mesh):
    in_specs = (
        P("grp", None, None, "ty", "tx"),
        P("ty", "tx"),
        P("ty", "tx"),
        P("ty", "tx"),
        P(),
        P(),
    )
    out_specs = P("grp", None, None, "ty", "tx")
    return jax.shard_map(local, mesh=mesh, in_specs=in_specs, out_specs=out_specs, check_vma=False)
```

```python
import functools

import jax
import jax.numpy as jnp
from jax import lax
from jax.experimental import pallas as pl
from jax.experimental.pallas import tpu as pltpu
from jax.sharding import PartitionSpec as P

STEPS = 2
NF = 23
NT = 19
NZ = 32
CH = 8
NK = NZ // CH
MESH = pl.DeviceIdType.MESH
F32 = jnp.float32

integration_interval = 0.1
tracer_step = 0.08
coriolis = 0.8
barotropic_gradient_coefficient = 0.1
water_extinction = 0.04
layer_depth = 0.05
growth_peak = 2.0
half_light = 0.5
ratio_floor = 0.01

DIAGS = ((-1, -1), (-1, 1), (1, -1), (1, 1))


def lanes(shape):
    return lax.broadcasted_iota(jnp.int32, shape, len(shape) - 1)


def roll(x, shift):
    return pltpu.roll(x, shift % 128 if isinstance(shift, int) else shift, x.ndim - 1)


def cumulative(x):
    n = x.shape[0]
    level = lax.broadcasted_iota(jnp.int32, x.shape, 0)
    d = 1
    while d < n:
        x = x + jnp.where(level >= d, pltpu.roll(x, d, 0), 0.0)
        d *= 2
    return x


def inverse(x):
    r = pl.reciprocal(x, approx=True)
    return r * (2.0 - x * r)


def kernel(
    x, land_in, bottom_in, shortwave_in, absorb_in, reaction_in, out,
    V, H, PS, PT, PD, ADV, CO, ZC, ZS, D, DH, SS, ST, KD, land, bottom, shortwave, absorb, reaction,
    lsem, psem, row_s, row_r, col_s, col_r, diag_s, diag_r, dyn_s, dyn_r, tra_s, tra_r, ors, orr, ocs, ocr,
):
    grp, ty, tx = lax.axis_index("grp"), lax.axis_index("ty"), lax.axis_index("tx")
    nty, ntx = lax.axis_size("ty"), lax.axis_size("tx")
    has_y = (ty > 0, ty < nty - 1)
    has_x = (tx > 0, tx < ntx - 1)
    step_of = (-1, 1)

    def has_diag(i):
        a, b = DIAGS[i]
        return has_y[(a + 1) // 2] & has_x[(b + 1) // 2]

    barrier = pltpu.get_barrier_semaphore()
    count = jnp.int32(1)
    pl.semaphore_signal(barrier, inc=1, device_id={"grp": 1 - grp}, device_id_type=MESH)
    for d in range(2):
        count = count + has_y[d].astype(jnp.int32) + has_x[d].astype(jnp.int32)

        @pl.when(has_y[d])
        def _():
            pl.semaphore_signal(barrier, inc=1, device_id={"ty": ty + step_of[d]}, device_id_type=MESH)

        @pl.when(has_x[d])
        def _():
            pl.semaphore_signal(barrier, inc=1, device_id={"tx": tx + step_of[d]}, device_id_type=MESH)

    load = pltpu.make_async_copy(x, V.at[0], lsem.at[0])
    load.start()
    small = [
        pltpu.make_async_copy(source, to, psem.at[i])
        for i, (source, to) in enumerate(
            (
                (land_in, land),
                (bottom_in, bottom),
                (shortwave_in, shortwave),
                (absorb_in, absorb),
                (reaction_in, reaction),
            )
        )
    ]
    for copy in small:
        copy.start()

    def fill(ref, n):
        def body(i, c):
            ref[i] = jnp.zeros(ref.shape[1:], F32)
            return c

        lax.fori_loop(0, n, body, 0)

    lane8 = lanes((CH, 128))
    four8 = lane8 % 4
    first, last = lane8 == 0, lane8 == 127

    def tracer_side():
        n_diag = jnp.int32(0)
        for i in range(4):
            n_diag = n_diag + has_diag(i).astype(jnp.int32)

            @pl.when(has_diag(i))
            def _():
                a, b = DIAGS[i]
                pl.semaphore_signal(barrier, inc=1, device_id={"ty": ty + a, "tx": tx + b}, device_id_type=MESH)

            @pl.when(jnp.logical_not(has_diag(i)))
            def _():
                for s in range(STEPS):
                    PD[s, i] = jnp.zeros(PD.shape[2:], F32)

        for d in range(2):
            @pl.when(jnp.logical_not(has_y[d]))
            def _():
                for s in range(STEPS):
                    fill(H.at[s, d], NF)

            @pl.when(jnp.logical_not(has_x[d]))
            def _():
                for s in range(STEPS):
                    fill(PT.at[s, d], 2)

        def row_copy(s, d, k, part):
            lo, n = ((0, 2), (4, NT))[part]
            rows = pl.ds(pl.multiple_of(k * 16, 16), 16) if part else pl.ds(0, 2 * NZ)
            src = (x if s == 0 else V.at[s]).at[pl.ds(lo, n), rows]
            return pltpu.make_async_remote_copy(
                src_ref=src,
                dst_ref=H.at[s, 1 - d, pl.ds(lo, n), rows],
                send_sem=row_s.at[s, d, k, part],
                recv_sem=row_r.at[s, 1 - d, k, part],
                device_id={"ty": ty + step_of[d]},
                device_id_type=MESH,
            )

        def row_arrival(s, d, k, part):
            lo, n = ((0, 2), (4, NT))[part]
            rows = pl.ds(pl.multiple_of(k * 16, 16), 16) if part else pl.ds(0, 2 * NZ)
            return pltpu.make_async_remote_copy(
                src_ref=V.at[s, pl.ds(lo, n), rows],
                dst_ref=H.at[s, d, pl.ds(lo, n), rows],
                send_sem=row_s.at[s, d, k, part],
                recv_sem=row_r.at[s, d, k, part],
                device_id={"ty": ty + step_of[d]},
                device_id_type=MESH,
            )

        def col_copy(s, d, k, arrival=False):
            lev = pl.ds(pl.multiple_of(k * CH, CH), CH)
            to = d if arrival else 1 - d
            return pltpu.make_async_remote_copy(
                src_ref=PS.at[s, :, lev],
                dst_ref=PT.at[s, to, :, lev],
                send_sem=col_s.at[s, d, k],
                recv_sem=col_r.at[s, to, k],
                device_id={"tx": tx + step_of[d]},
                device_id_type=MESH,
            )

        def diag_copy(s, i, k, arrival=False):
            a, b = DIAGS[i]
            lev = pl.ds(pl.multiple_of(k * CH, CH), CH)
            to = i if arrival else 3 - i
            return pltpu.make_async_remote_copy(
                src_ref=PS.at[s, (a + 1) // 2, lev],
                dst_ref=PD.at[s, to, lev],
                send_sem=diag_s.at[s, i, k],
                recv_sem=diag_r.at[s, to, k],
                device_id={"ty": ty + a, "tx": tx + b},
                device_id_type=MESH,
            )

        def tracer_rows(s, k, act):
            for d in range(2):
                @pl.when(has_y[d])
                def _():
                    act(s, d, k, 1)

        def velocity_rows(s, act):
            for d in range(2):
                @pl.when(has_y[d])
                def _():
                    act(s, d, 0, 0)

        def each_row(s, k, act):
            for d in range(2):
                @pl.when(has_y[d] & (k == 0))
                def _():
                    act(s, d, 0, 0)

                @pl.when(has_y[d])
                def _():
                    act(s, d, k, 1)

        def send_rows(s, k):
            each_row(s, k, lambda *a: row_copy(*a).start())

        def send_edges(s, k):
            for d in range(2):
                @pl.when(has_x[d])
                def _():
                    col_copy(s, d, k).start()
            for i in range(4):
                @pl.when(has_diag(i))
                def _():
                    diag_copy(s, i, k).start()

        def receive(s, k):
            for d in range(2):
                @pl.when(has_x[d])
                def _():
                    col_copy(s, d, k, True).wait_recv()
            for i in range(4):
                @pl.when(has_diag(i))
                def _():
                    diag_copy(s, i, k, True).wait_recv()
            each_row(s, k, lambda *a: row_arrival(*a).wait_recv())

        def sent(s, k):
            each_row(s, k, lambda *a: row_copy(*a).wait_send())
            for d in range(2):
                @pl.when(has_x[d])
                def _():
                    col_copy(s, d, k).wait_send()
            for i in range(4):
                @pl.when(has_diag(i))
                def _():
                    diag_copy(s, i, k).wait_send()

        def tracers_over(k):
            rows = pl.ds(pl.multiple_of(k * 16, 16), 16)
            return pltpu.make_async_remote_copy(
                src_ref=V.at[1, pl.ds(4, NT), rows],
                dst_ref=V.at[2, pl.ds(4, NT), rows],
                send_sem=tra_s.at[k],
                recv_sem=tra_r.at[k],
                device_id={"grp": 1 - grp},
                device_id_type=MESH,
            )

        def store_out(k):
            rows = pl.ds(pl.multiple_of(k * 16, 16), 16)
            return pltpu.make_async_copy(V.at[2, pl.ds(4, NT), rows], out.at[pl.ds(4, NT), rows], lsem.at[1 + k])

        def pack(s, start, count):
            lane = lanes((count, 128))
            quarter = lane // 4

            def body(f, rows):
                shift = 4 * f + 2
                return tuple(
                    jnp.where(quarter == f, roll(V[s, f, pl.ds(2 * start + r, count, 2), :], shift), rows[r])
                    for r in range(2)
                )

            zero = jnp.zeros((count, 128), F32)
            packed = lax.fori_loop(0, NF, body, (zero, zero), unroll=True)
            for r in range(2):
                PS[s, r, pl.ds(start, count), :] = packed[r]

        def chunk(s, k, carry):
            base = k * 16
            lev = pl.ds(pl.multiple_of(k * CH, CH), CH)

            def row(f, r):
                at = pl.ds(base + r % 2, CH, 2)
                if r < 0:
                    return H[s, 0, f, at, :]
                if r > 1:
                    return H[s, 1, f, at, :]
                return V[s, f, at, :]

            y_lo = jnp.where(has_y[0], 0.02, 0.0).astype(F32)
            y_hi = jnp.where(has_y[1], 0.02, 0.0).astype(F32)
            x_lo = jnp.where(has_x[0], 0.02, 0.0).astype(F32)
            x_hi = jnp.where(has_x[1], 0.02, 0.0).astype(F32)
            right = four8 == 1
            left = four8 == 2

            own = [PS[s, r, lev, :] for r in range(2)]
            low = [PD[s, 0, lev, :], PT[s, 0, 0, lev, :], PT[s, 0, 1, lev, :], PD[s, 2, lev, :]]
            high = [PD[s, 1, lev, :], PT[s, 1, 0, lev, :], PT[s, 1, 1, lev, :], PD[s, 3, lev, :]]
            mid = [jnp.where(right, roll(high[i], -1), roll(low[i], 1)) for i in range(4)]
            for i in range(4):
                ZC[i] = mid[i]
            north = [jnp.where(right, roll(high[1 + r], -2), own[r]) for r in range(2)]
            south = [jnp.where(right, own[r], roll(low[1 + r], 2)) for r in range(2)]

            def spread(value, f):
                value = jnp.where(lane8 // 4 == f, value, 0.0)
                for d in (4, 8, 16, 32, 64):
                    value = value + roll(value, d)
                return value

            def face(q, a, b):
                anti = jnp.abs(q) * (b - a)
                return anti, q * (a + b) - anti

            def bounds(centre, others):
                hi = lo = centre
                for o in others:
                    hi, lo = jnp.maximum(hi, o), jnp.minimum(lo, o)
                return hi, lo

            def gains(w, e, n, so):
                gain_in = (jnp.maximum(w, 0.0) - jnp.minimum(e, 0.0)) + (jnp.maximum(so, 0.0) - jnp.minimum(n, 0.0))
                gain_out = (jnp.maximum(e, 0.0) - jnp.minimum(w, 0.0)) + (jnp.maximum(n, 0.0) - jnp.minimum(so, 0.0))
                return gain_in, gain_out

            def ratio(gain, room):
                return jnp.minimum(gain, jnp.maximum(room, 0.0)) * inverse(
                    jnp.maximum(gain, ratio_floor * tracer_step)
                )

            u_mid = [spread(m, 0) for m in mid]
            q_rows = [
                (u_mid[0] + u_mid[1]) * y_lo,
                (u_mid[1] + u_mid[2]) * 0.02,
                (u_mid[2] + u_mid[3]) * y_hi,
            ]
            faces = [face(q_rows[i], mid[i], mid[i + 1]) for i in range(3)]
            for r in range(2):
                v_mid = spread(mid[1 + r], 1)
                q_n = (v_mid + spread(north[r], 1)) * jnp.where(left, x_lo, 0.02)
                q_s = (v_mid + spread(south[r], 1)) * jnp.where(right, x_hi, 0.02)
                a_n, l_n = face(q_n, mid[1 + r], north[r])
                a_s, l_s = face(q_s, south[r], mid[1 + r])
                a_w, l_w = faces[r]
                a_e, l_e = faces[r + 1]
                lowered = mid[1 + r] - (l_e - l_w + l_n - l_s)
                hi, lo = bounds(mid[1 + r], (mid[r], mid[2 + r], north[r], south[r]))
                gain_in, gain_out = gains(a_w, a_e, a_n, a_s)
                take_in = (right & (a_s >= 0.0)) | (jnp.logical_not(right) & (a_n < 0.0))
                gain = jnp.where(take_in, gain_in, gain_out)
                room = jnp.where(take_in, hi - lowered, lowered - lo)
                ZS[r] = ratio(gain, room)

            u = [row(0, r) for r in range(-2, 4)]
            for i, scale in enumerate((0.02, y_lo, 0.02, y_hi, 0.02)):
                CO[i] = (u[i] + u[i + 1]) * scale
            for i in range(4):
                v = row(1, i - 1)
                side = roll(mid[i], 126 - 4)
                CO[5 + i] = (v + jnp.where(last, side, roll(v, -1))) * jnp.where(last, x_hi, 0.02)
                CO[9 + i] = (v + jnp.where(first, side, roll(v, 1))) * jnp.where(first, x_lo, 0.02)

            def transport(t, extinction):
                f = t + 4
                c = [row(f, r) for r in range(-2, 4)]
                turn = 126 - 4 * f
                fe = [face(CO[i], c[i], c[i + 1]) for i in range(5)]
                lowered, ratio_in, ratio_out, an, as_ = {}, {}, {}, {}, {}
                for i in range(1, 5):
                    side = roll(ZC[i - 1], turn)
                    c_n = jnp.where(last, side, roll(c[i], -1))
                    c_s = jnp.where(first, side, roll(c[i], 1))
                    a_n, l_n = face(CO[4 + i], c[i], c_n)
                    a_s, l_s = face(CO[8 + i], c_s, c[i])
                    a_w, l_w = fe[i - 1]
                    a_e, l_e = fe[i]
                    low_c = c[i] - (l_e - l_w + l_n - l_s)
                    hi, lo = bounds(c[i], (c[i - 1], c[i + 1], c_n, c_s))
                    gain_in, gain_out = gains(a_w, a_e, a_n, a_s)
                    room_in, room_out = hi - low_c, low_c - lo
                    if i in (1, 4):
                        take_in = a_e < 0.0 if i == 1 else a_w >= 0.0
                        ratio_in[i] = ratio(
                            jnp.where(take_in, gain_in, gain_out), jnp.where(take_in, room_in, room_out)
                        )
                    else:
                        lowered[i], an[i], as_[i] = low_c, a_n, a_s
                        ratio_in[i] = ratio(gain_in, room_in)
                        ratio_out[i] = ratio(gain_out, room_out)
                a = fe[1][0]
                f_lo = a * jnp.minimum(ratio_in[1], jnp.where(a >= 0.0, ratio_in[2], ratio_out[2]))
                a = fe[2][0]
                f_mid = a * jnp.where(
                    a >= 0.0,
                    jnp.minimum(ratio_in[3], ratio_out[2]),
                    jnp.minimum(ratio_in[2], ratio_out[3]),
                )
                a = fe[3][0]
                f_hi = a * jnp.minimum(jnp.where(a >= 0.0, ratio_out[3], ratio_in[3]), ratio_in[4])
                result = []
                for i, f_w, f_e in ((2, f_lo, f_mid), (3, f_mid, f_hi)):
                    side = roll(ZS[i - 2], turn)
                    a_n, a_s = an[i], as_[i]
                    up = a_n >= 0.0
                    mine = jnp.where(up, ratio_out[i], ratio_in[i])
                    other = jnp.where(up, roll(ratio_in[i], -1), roll(ratio_out[i], -1))
                    f_n = a_n * jnp.minimum(mine, jnp.where(last, side, other))
                    at_rim = a_s * jnp.minimum(side, jnp.where(a_s >= 0.0, ratio_in[i], ratio_out[i]))
                    f_s = jnp.where(first, at_rim, roll(f_n, 1))
                    advected = lowered[i] - (f_e - f_w + f_n - f_s)
                    ADV[t, i - 2] = advected
                    result.append(extinction[i - 2] + absorb[t] * advected)
                return tuple(result)

            base_light = jnp.full((CH, 128), water_extinction, F32)
            extinction = lax.fori_loop(0, NT, transport, (base_light, base_light), unroll=True)

            level = k * CH + lax.broadcasted_iota(jnp.int32, (CH, 128), 0)
            wet, growth, carries = [], [], []
            for r in range(2):
                total = cumulative(extinction[r]) + carry[r]
                carries.append(carry[r] + jnp.sum(extinction[r], axis=0, keepdims=True))
                below = shortwave[pl.ds(r, 1), :] * jnp.exp(-layer_depth * total)
                sea = (land[pl.ds(r, 1), :] == 1) & (level < bottom[pl.ds(r, 1), :])
                wet.append(jnp.where(sea, 1.0, 0.0))
                grow = (
                    growth_peak
                    * jnp.exp(0.063 * row(2, r))
                    * below
                    / (below + half_light)
                    * (1.0 + 0.2 * jnp.tanh(row(3, r)))
                )
                growth.append(wet[r] * (tracer_step * grow))

            def react(o, c):
                for r in range(2):
                    mixed = reaction[o, 0] * ADV[0, r]
                    for t in range(1, NT):
                        mixed = mixed + reaction[o, t] * ADV[t, r]
                    V[s + 1, o + 4, pl.ds(base + r, CH, 2), :] = wet[r] * ADV[o, r] + growth[r] * mixed
                return c

            lax.fori_loop(0, NT, react, 0, unroll=True)
            return tuple(carries)

        dynamics_in = pltpu.make_async_remote_copy(
            src_ref=V.at[1, pl.ds(0, 4)],
            dst_ref=V.at[1, pl.ds(0, 4)],
            send_sem=dyn_s,
            recv_sem=dyn_r,
            device_id={"grp": 1 - grp},
            device_id_type=MESH,
        )
        dynamics_out = pltpu.make_async_copy(V.at[1, pl.ds(0, 4)], out.at[pl.ds(0, 4)], lsem.at[0])

        load.wait()
        for copy in small:
            copy.wait()
        pack(0, 0, NZ)
        pl.semaphore_wait(barrier, count + n_diag)

        def begin(k, c):
            send_edges(0, k)
            return c

        lax.fori_loop(0, NK, begin, 0)
        lax.fori_loop(0, NK, lambda k, c: (send_rows(0, k), c)[1], 0)

        zero = jnp.zeros((1, 128), F32)

        def first_step(k, carry):
            receive(0, k)
            carry = chunk(0, k, carry)

            @pl.when(k == 0)
            def _():
                tracer_rows(1, k, lambda *a: row_copy(*a).start())
                dynamics_in.wait_recv()
                dynamics_out.start()
                velocity_rows(1, lambda *a: row_copy(*a).start())

            pack(1, k * CH, CH)
            send_edges(1, k)

            @pl.when(k > 0)
            def _():
                tracer_rows(1, k, lambda *a: row_copy(*a).start())

            tracers_over(k).start()
            return carry

        lax.fori_loop(0, NK, first_step, (zero, zero))

        def second_step(k, carry):
            receive(1, k)
            carry = chunk(1, k, carry)
            store_out(k).start()
            return carry

        lax.fori_loop(0, NK, second_step, (zero, zero))

        def finish(k, c):
            sent(0, k)
            sent(1, k)
            tracers_over(k).wait_send()
            store_out(k).wait()
            return c

        lax.fori_loop(0, NK, finish, 0)
        dynamics_out.wait()

    def ocean_side():
        for d in range(2):
            @pl.when(jnp.logical_not(has_y[d]))
            def _():
                for s in range(STEPS):
                    fill(DH.at[s, d], 4)

            @pl.when(jnp.logical_not(has_x[d]))
            def _():
                for s in range(STEPS):
                    fill(ST.at[s, d], 2)

        lane = lanes((NZ, 128))
        four, quarter = lane % 4, lane // 4
        first_z, last_z = lane == 0, lane == 127

        def row_copy(s, d, arrival=False):
            to = d if arrival else 1 - d
            return pltpu.make_async_remote_copy(
                src_ref=D.at[s, d],
                dst_ref=DH.at[s, to],
                send_sem=ors.at[s, d],
                recv_sem=orr.at[s, to],
                device_id={"ty": ty + step_of[d]},
                device_id_type=MESH,
            )

        def col_copy(s, d, arrival=False):
            to = d if arrival else 1 - d
            return pltpu.make_async_remote_copy(
                src_ref=SS.at[s],
                dst_ref=ST.at[s, to],
                send_sem=ocs.at[s, d],
                recv_sem=ocr.at[s, to],
                device_id={"tx": tx + step_of[d]},
                device_id_type=MESH,
            )

        def exchange(s, act):
            for d in range(2):
                @pl.when(has_y[d])
                def _():
                    act(row_copy, s, d)

                @pl.when(has_x[d])
                def _():
                    act(col_copy, s, d)

        def pack(s):
            for r in range(2):
                packed = jnp.zeros((NZ, 128), F32)
                for f in range(4):
                    packed = jnp.where(quarter == f, roll(D[s, r, f], 4 * f + 2), packed)
                SS[s, r] = packed

        def light(ref):
            def body(t, acc):
                return acc + absorb[t] * ref[t + 4]

            KD[...] = lax.fori_loop(0, NT, body, jnp.full((2 * NZ, 128), water_extinction, F32))

        def update(s):
            level = lax.broadcasted_iota(jnp.int32, (NZ, 128), 0)
            for r in range(2):
                side = jnp.where(four == 1, roll(ST[s, 1, r], -1), roll(ST[s, 0, r], 1))
                own, lap, e_w, n_s = [], [], [], []
                for f in range(4):
                    c = D[s, r, f]
                    w = DH[s, 0, f] if r == 0 else D[s, 0, f]
                    e = DH[s, 1, f] if r == 1 else D[s, 1, f]
                    rim = roll(side, 126 - 4 * f)
                    n = jnp.where(last_z, rim, roll(c, -1))
                    so = jnp.where(first_z, rim, roll(c, 1))
                    own.append(c)
                    lap.append((e + w + n + so) - 4.0 * c)
                    e_w.append(e - w)
                    n_s.append(n - so)
                half = 0.5 * barotropic_gradient_coefficient
                grad_east = cumulative((-0.2 * e_w[2] + 0.8 * e_w[3]) * half)
                grad_north = cumulative((-0.2 * n_s[2] + 0.8 * n_s[3]) * half)
                extinction = KD[pl.ds(r, NZ, 2), :]
                below = shortwave[pl.ds(r, 1), :] * jnp.exp(-layer_depth * cumulative(extinction))
                above = below * jnp.exp(layer_depth * extinction)
                sea = (land[pl.ds(r, 1), :] == 1) & (level < bottom[pl.ds(r, 1), :])
                wet = jnp.where(sea, 1.0, 0.0)
                step = integration_interval
                new = (
                    own[0] + step * (coriolis * own[1] - grad_east + lap[0]),
                    own[1] + step * (-coriolis * own[0] - grad_north + lap[1]),
                    own[2] + step * (lap[2] + (above - below) / layer_depth),
                    own[3] + step * lap[3],
                )
                for f in range(4):
                    value = wet * new[f]
                    V[s + 1, f, pl.ds(r, NZ, 2), :] = value
                    if s + 1 < STEPS:
                        D[s + 1, r, f] = value

        dynamics_over = pltpu.make_async_remote_copy(
            src_ref=V.at[1, pl.ds(0, 4)],
            dst_ref=V.at[1, pl.ds(0, 4)],
            send_sem=dyn_s,
            recv_sem=dyn_r,
            device_id={"grp": 1 - grp},
            device_id_type=MESH,
        )

        def tracers_in(k):
            rows = pl.ds(pl.multiple_of(k * 16, 16), 16)
            return pltpu.make_async_remote_copy(
                src_ref=V.at[1, pl.ds(4, NT), rows],
                dst_ref=V.at[2, pl.ds(4, NT), rows],
                send_sem=tra_s.at[k],
                recv_sem=tra_r.at[k],
                device_id={"grp": 1 - grp},
                device_id_type=MESH,
            )

        load.wait()
        for copy in small:
            copy.wait()
        for r in range(2):
            for f in range(4):
                D[0, r, f] = V[0, f, pl.ds(r, NZ, 2), :]
        pack(0)
        pl.semaphore_wait(barrier, count)
        exchange(0, lambda copy, s, d: copy(s, d).start())
        light(V.at[0])
        exchange(0, lambda copy, s, d: copy(s, d, True).wait_recv())
        update(0)
        dynamics_over.start()
        pack(1)
        exchange(1, lambda copy, s, d: copy(s, d).start())

        def tracers_out(k):
            rows = pl.ds(pl.multiple_of(k * 16, 16), 16)
            return pltpu.make_async_copy(V.at[2, pl.ds(4, NT), rows], out.at[pl.ds(4, NT), rows], lsem.at[1 + k])

        def arrive(k, c):
            tracers_in(k).wait_recv()
            tracers_out(k).start()
            return c

        lax.fori_loop(0, NK, arrive, 0)
        light(V.at[2])
        exchange(1, lambda copy, s, d: copy(s, d, True).wait_recv())
        update(1)
        dynamics_out = pltpu.make_async_copy(V.at[2, pl.ds(0, 4)], out.at[pl.ds(0, 4)], lsem.at[0])
        dynamics_out.start()
        exchange(0, lambda copy, s, d: copy(s, d).wait_send())
        exchange(1, lambda copy, s, d: copy(s, d).wait_send())
        dynamics_over.wait_send()

        def finish(k, c):
            tracers_out(k).wait()
            return c

        lax.fori_loop(0, NK, finish, 0)
        dynamics_out.wait()

    pl.when(grp == 1)(tracer_side)
    pl.when(grp == 0)(ocean_side)


def local(coupled_state, land_mask, bottom_level, shortwave, absorb, reaction):
    x = coupled_state.reshape(NF, 2 * NZ, 128)
    hbm = pl.BlockSpec(memory_space=pltpu.HBM)
    dma = pltpu.SemaphoreType.DMA
    y = pl.pallas_call(
        kernel,
        out_shape=jax.ShapeDtypeStruct((NF, 2 * NZ, 128), F32),
        in_specs=[hbm] * 6,
        out_specs=hbm,
        scratch_shapes=[
            pltpu.VMEM((STEPS + 1, NF, 2 * NZ, 128), F32),
            pltpu.VMEM((STEPS, 2, NF, 2 * NZ, 128), F32),
            pltpu.VMEM((STEPS, 2, NZ, 128), F32),
            pltpu.VMEM((STEPS, 2, 2, NZ, 128), F32),
            pltpu.VMEM((STEPS, 4, NZ, 128), F32),
            pltpu.VMEM((NT, 2, CH, 128), F32),
            pltpu.VMEM((13, CH, 128), F32),
            pltpu.VMEM((4, CH, 128), F32),
            pltpu.VMEM((2, CH, 128), F32),
            pltpu.VMEM((STEPS, 2, 4, NZ, 128), F32),
            pltpu.VMEM((STEPS, 2, 4, NZ, 128), F32),
            pltpu.VMEM((STEPS, 2, NZ, 128), F32),
            pltpu.VMEM((STEPS, 2, 2, NZ, 128), F32),
            pltpu.VMEM((2 * NZ, 128), F32),
            pltpu.VMEM((2, 128), jnp.int32),
            pltpu.VMEM((2, 128), jnp.int32),
            pltpu.VMEM((2, 128), F32),
            pltpu.SMEM((NT,), F32),
            pltpu.SMEM((NT, NT), F32),
            dma((1 + NK,)),
            dma((5,)),
            dma((STEPS, 2, NK, 2)),
            dma((STEPS, 2, NK, 2)),
            dma((STEPS, 2, NK)),
            dma((STEPS, 2, NK)),
            dma((STEPS, 4, NK)),
            dma((STEPS, 4, NK)),
            dma,
            dma,
            dma((NK,)),
            dma((NK,)),
            dma((STEPS, 2)),
            dma((STEPS, 2)),
            dma((STEPS, 2)),
            dma((STEPS, 2)),
        ],
        compiler_params=pltpu.CompilerParams(
            collective_id=0, has_side_effects=True
        ),
    )(x, land_mask, bottom_level, shortwave, absorb, reaction)
    return y.reshape(1, NF, NZ, 2, 128)


def solution(mesh):
    in_specs = (
        P("grp", None, None, "ty", "tx"),
        P("ty", "tx"),
        P("ty", "tx"),
        P("ty", "tx"),
        P(),
        P(),
    )
    out_specs = P("grp", None, None, "ty", "tx")
    return jax.shard_map(local, mesh=mesh, in_specs=in_specs, out_specs=out_specs, check_vma=False)
```
